1024 devices in a mesh: row: 16 (over z), col: 32 (over y, x), depth: 2 (over core).
Axes of the slice: x: 4, y: 8, z: 16, core: 2. Of those that a mesh axis runs over, the one named last changes fastest.
Arguments:
- density: bfloat16 [1024, 27, 64, 64], P(('row', 'col', 'depth')), may hold values from -1.296875 to 1.296875
- pattern: int32 [1024, 27], P(('row', 'col', 'depth')), may hold values 0 or 1
Outputs:
- square: bfloat16 [1024, 27, 64, 64], P(('row', 'col', 'depth'))
The draws below stay inside these ranges and needn't reach their ends.
All inputs are finite; a program needn't handle non-finite values. No bound on the sum of `pattern` on one device may be relied on, other than what follows from the above.
Results may differ from the reference program's by a relative error of at most 0.001.
Values may be sent and summed in bfloat16 or wider, within the bound.
A program may use at most 64 MiB of HBM per device.

```python
import jax
import jax.numpy as jnp
import numpy as np
from jax import lax

BLOCK = 64
NEIGHBOURS = 27
ROWS_A = 16
ROWS_B = 32
LAYERS = 2
GROUPS = 1024


def plant(entries, rng, low, high):
    dims = entries.shape
    index_at = [jax.random.randint(jax.random.fold_in(rng, axis), (), 0, dims[axis]) for axis in range(len(dims))]
    entries = entries.at[tuple(index_at)].set(low)
    longest = dims.index(max(dims))
    index_at[longest] = (index_at[longest] + 1) % dims[longest]
    return entries.at[tuple(index_at)].set(high)


def level_of(rng, shape, shards, least, largest):
    gain = 1.0
    for position, shards_of in shards:
        heights = jax.random.uniform(jax.random.fold_in(jax.random.fold_in(rng, 6), position), (shards_of,), jnp.float32, least / len(shards), largest / len(shards))
        gain = gain * jnp.repeat(jnp.exp(heights), shape[position] // shards_of).reshape((-1,) + (1,) * (len(shape) - 1 - position))
    return gain


def gaussian(key, extent, spread, most, split=(), kind=jnp.bfloat16):
    result = jax.random.normal(key, extent, jnp.float32) * spread
    if len(split) > 0:
        result = level_of(key, extent, split, -0.22, 0.18) * result
    return jnp.clip(result, min=-most, max=most).astype(kind)


def setup_inputs(seed: int = 0) -> dict:
    key_of = jax.random.split(jax.random.key(seed), 3)
    density = gaussian(key_of[0], (GROUPS, NEIGHBOURS, BLOCK, BLOCK), 0.22, 1.296875, ((0, 1024),))
    pattern = plant((jax.random.randint(key_of[1], (GROUPS, NEIGHBOURS), 0, 4) < 3).astype(jnp.int32), jax.random.fold_in(key_of[1], 1), 0, 1)
    return {"density": density, "pattern": pattern}


def slot_pairs():
    firsts = []
    seconds = []
    targets = []
    for first_slot in range(27):
        a_one, b_one, z_one = first_slot // 9 - 1, (first_slot // 3) % 3 - 1, first_slot % 3 - 1
        for second_slot in range(27):
            a_two, b_two, z_two = second_slot // 9 - 1, (second_slot // 3) % 3 - 1, second_slot % 3 - 1
            a_sum, b_sum, z_sum = a_one + a_two, b_one + b_two, z_one + z_two
            if max(abs(a_sum), abs(b_sum), abs(z_sum)) > 1:
                continue
            firsts.append(first_slot)
            seconds.append(second_slot)
            targets.append(9 * (a_sum + 1) + 3 * (b_sum + 1) + z_sum + 1)
    onehot = np.zeros((len(targets), 27), np.float32)
    onehot[np.arange(len(targets)), np.array(targets)] = 1.0
    return np.array(firsts, np.int32), np.array(seconds, np.int32), onehot


def reference(density, pattern):
    groups = ROWS_A * ROWS_B * LAYERS
    group_ids = jnp.arange(groups, dtype=jnp.int32)
    a_site = group_ids // (ROWS_B * LAYERS)
    b_site = (group_ids // LAYERS) % ROWS_B
    z_site = group_ids % LAYERS
    slot_ids = jnp.arange(27, dtype=jnp.int32)
    a_step = slot_ids // 9 - 1
    b_step = (slot_ids // 3) % 3 - 1
    z_step = slot_ids % 3 - 1
    a_near = (a_site[:, None] + a_step[None, :]) % ROWS_A
    b_near = (b_site[:, None] + b_step[None, :]) % ROWS_B
    z_near = z_site[:, None] + z_step[None, :]
    inside = (z_near >= 0) & (z_near < LAYERS)
    present = jnp.where(inside, pattern, 0).astype(jnp.int32)
    neighbour = ((a_near * ROWS_B + b_near) * LAYERS + jnp.clip(z_near, 0, LAYERS - 1)).astype(jnp.int32)
    blocks = density * present.astype(jnp.bfloat16)[:, :, None, None]
    firsts, seconds, onehot = slot_pairs()
    firsts = jnp.asarray(firsts)
    seconds = jnp.asarray(seconds)
    onehot = jnp.asarray(onehot)

    def one_batch(labels):
        left_blocks = blocks[labels][:, firsts].astype(jnp.float32)
        partner_rows = neighbour[labels][:, firsts]
        right_blocks = blocks[partner_rows, seconds[None, :]].astype(jnp.float32)
        products = jnp.einsum("ptab,ptbc->ptac", left_blocks, right_blocks)
        return jnp.einsum("ptac,ts->psac", products, onehot)

    batch_rows = 8 if groups % 8 == 0 else 1
    batches = group_ids.reshape(groups // batch_rows, batch_rows)
    summed = lax.map(one_batch, batches).reshape(groups, 27, BLOCK, BLOCK)
    return (summed * present.astype(jnp.float32)[:, :, None, None]).astype(jnp.bfloat16)
```

```python
import functools

import jax
import jax.numpy as jnp
from jax import lax
from jax.experimental import pallas as pl
from jax.experimental.pallas import tpu as pltpu
from jax.sharding import PartitionSpec as P

MESH = pl.DeviceIdType.MESH
STEPS = [(a, b) for a in (-1, 0, 1) for b in (-1, 0, 1)]
CENTRE = 4
AWAY = [0, 2, 6, 8, 1, 7, 3, 5]


def pairs_of(t):
    a, b = STEPS[t]
    found = []
    for target, (goal_a, goal_b) in enumerate(STEPS):
        rest = (goal_a - a, goal_b - b)
        if rest in STEPS:
            found.append((target, STEPS.index(rest)))
    return found


def tiles_of(t):
    return -(-len(pairs_of(t)) // 2)


def kernel(
    density_hbm,
    pattern_ref,
    out_ref,
    density,
    kept,
    left,
    outgoing,
    incoming,
    total,
    ship,
    landed,
    load_sem,
    left_sems,
    send_sems,
    recv_sems,
    ship_sems,
):
    rows, cols = lax.axis_size("row"), lax.axis_size("col")
    a, b, z = lax.axis_index("row"), lax.axis_index("col"), lax.axis_index("depth")
    other = 1 - z
    size = density.shape[-1]

    load = pltpu.make_async_copy(density_hbm.at[0], density, load_sem)
    load.start()

    def device(t, layer):
        step_a, step_b = STEPS[t]
        return {
            "row": lax.rem(a - step_a + rows, rows),
            "col": lax.rem(b - step_b + cols, cols),
            "depth": layer,
        }

    barrier = pltpu.get_barrier_semaphore()
    for t in AWAY:
        for layer in range(2):
            pl.semaphore_signal(
                barrier, inc=1, device_id=device(t, layer), device_id_type=MESH
            )
    pl.semaphore_signal(
        barrier, inc=1, device_id=device(CENTRE, other), device_id_type=MESH
    )
    load.wait()

    for slot in range(9):
        for layer in range(2):
            place = 3 * slot + 1 + layer - z
            block = density[place]
            kept[layer, slot] = jnp.where(
                pattern_ref[0, place] != 0, block, jnp.zeros_like(block)
            )
    for slot in range(9):
        left[z, slot] = jnp.concatenate([kept[0, slot], kept[1, slot]], axis=1)
    for t in AWAY + [CENTRE]:
        slots = [slot for _, slot in pairs_of(t)]
        for layer in range(2):
            for j in range(tiles_of(t)):
                first = kept[layer, slots[2 * j]]
                if 2 * j + 1 < len(slots):
                    second = kept[layer, slots[2 * j + 1]]
                else:
                    second = jnp.zeros_like(first)
                outgoing[t, layer, j] = jnp.concatenate([first, second], axis=1)
    for j in range(tiles_of(CENTRE)):
        incoming[CENTRE, z, j] = outgoing[CENTRE, z, j]

    pl.semaphore_wait(barrier, 17)

    copies = []

    def send(src, dst, send_sem, recv_sem, target):
        copy = pltpu.make_async_remote_copy(
            src_ref=src,
            dst_ref=dst,
            send_sem=send_sem,
            recv_sem=recv_sem,
            device_id=target,
            device_id_type=MESH,
        )
        copy.start()
        copies.append(copy)
        return copy

    for t in AWAY:
        count = tiles_of(t)
        for layer in range(2):
            send(
                outgoing.at[t, layer, pl.ds(0, count)],
                incoming.at[t, z, pl.ds(0, count)],
                send_sems.at[t, layer],
                recv_sems.at[t, z],
                device(t, layer),
            )
    sibling = device(CENTRE, other)
    send(left.at[z], left.at[z], left_sems.at[0], left_sems.at[1], sibling)
    send(
        outgoing.at[CENTRE, other],
        incoming.at[CENTRE, z],
        send_sems.at[CENTRE, 0],
        recv_sems.at[CENTRE, z],
        sibling,
    )

    def arrived(ref, sem):
        pltpu.make_async_copy(ref, ref, sem).wait()

    def multiply(t, first):
        count = tiles_of(t)
        lhs = jnp.concatenate([left[0, t], left[1, t]], axis=0)
        tiles = [
            jnp.concatenate([incoming[t, 0, j], incoming[t, 1, j]], axis=0)
            for j in range(count)
        ]
        product = jnp.dot(
            lhs, jnp.concatenate(tiles, axis=1), preferred_element_type=jnp.float32
        )
        for place, (target, _) in enumerate(pairs_of(t)):
            part = product[:, place * size : (place + 1) * size]
            for layer in range(2):
                rows_of = part[layer * size : (layer + 1) * size]
                if first:
                    total[target, layer] = rows_of
                else:
                    total[target, layer] += rows_of

    arrived(left.at[other], left_sems.at[1])
    arrived(incoming.at[CENTRE, other], recv_sems.at[CENTRE, other])
    multiply(CENTRE, True)
    for t in AWAY:
        for layer in range(2):
            arrived(incoming.at[t, layer, pl.ds(0, tiles_of(t))], recv_sems.at[t, layer])
        multiply(t, False)

    for j in range(5):
        first = total[2 * j, other]
        second = total[2 * j + 1, other] if j < 4 else jnp.zeros_like(first)
        ship[j] = jnp.concatenate([first, second], axis=1).astype(ship.dtype)
    send(ship, landed, ship_sems.at[0], ship_sems.at[1], sibling)

    nothing = jnp.zeros((size, size), out_ref.dtype)
    for target in range(9):
        out_ref[0, 3 * target + 1 + z - other] = nothing
        place = 3 * target + 1
        out_ref[0, place] = jnp.where(
            pattern_ref[0, place] != 0, total[target, z].astype(out_ref.dtype), nothing
        )
    arrived(landed, ship_sems.at[1])
    for target in range(9):
        j, half = target // 2, target % 2
        block = landed[j][:, half * size : (half + 1) * size]
        place = 3 * target + 1 + other - z
        out_ref[0, place] = jnp.where(pattern_ref[0, place] != 0, block, nothing)
    for copy in copies:
        copy.wait_send()


def local(density, pattern):
    size = density.shape[-1]
    kind = density.dtype
    wide = 2 * size
    return pl.pallas_call(
        kernel,
        out_shape=jax.ShapeDtypeStruct(density.shape, kind),
        in_specs=[
            pl.BlockSpec(memory_space=pl.ANY),
            pl.BlockSpec(memory_space=pltpu.SMEM),
        ],
        out_specs=pl.BlockSpec(memory_space=pltpu.VMEM),
        scratch_shapes=[
            pltpu.VMEM((27, size, size), kind),
            pltpu.VMEM((2, 9, size, size), kind),
            pltpu.VMEM((2, 9, size, wide), kind),
            pltpu.VMEM((9, 2, 5, size, wide), kind),
            pltpu.VMEM((9, 2, 5, size, wide), kind),
            pltpu.VMEM((9, 2, size, size), jnp.float32),
            pltpu.VMEM((5, size, wide), kind),
            pltpu.VMEM((5, size, wide), kind),
            pltpu.SemaphoreType.DMA,
            pltpu.SemaphoreType.DMA((2,)),
            pltpu.SemaphoreType.DMA((9, 2)),
            pltpu.SemaphoreType.DMA((9, 2)),
            pltpu.SemaphoreType.DMA((2,)),
        ],
        compiler_params=pltpu.CompilerParams(
            collective_id=0,
            has_side_effects=True,
            vmem_limit_bytes=32 * 1024 * 1024,
        ),
    )(density, pattern)


def solution(mesh):
    placed = (P(("row", "col", "depth"), None, None, None), P(("row", "col", "depth"), None))
    return jax.shard_map(
        local,
        mesh=mesh,
        in_specs=placed,
        out_specs=P(("row", "col", "depth"), None, None, None),
        check_vma=False,
    )
```

```python
import jax
import jax.numpy as jnp
from jax import lax
from jax.experimental import pallas as pl
from jax.experimental.pallas import tpu as pltpu
from jax.sharding import PartitionSpec as P

MESH = pl.DeviceIdType.MESH
STEPS = [(a, b) for a in (-1, 0, 1) for b in (-1, 0, 1)]
CENTRE = 4
ROW_UP = [0, 2, 1]
COLUMN = [3, 5]
ROW_DOWN = [6, 7, 8]
AWAY = ROW_UP + COLUMN + ROW_DOWN

TILES = [
    ((1, -1), (1, 0)),
    ((-1, -1), (0, -1)),
    ((-1, 0), (0, 0)),
    ((-1, 1), (0, 1)),
    ((1, 0), (1, 1)),
    ((0, -1), (1, -1)),
    ((0, 0), (1, 0)),
    ((0, 1), (1, 1)),
]


def tiles_of(t):
    a, b = STEPS[t]
    if a == 0:
        return {-1: (2, 3), 0: (0, 5), 1: (0, 3)}[b]
    first = 5 if a == -1 else 1
    return {-1: (first + 1, 2), 0: (first, 3), 1: (first, 2)}[b]


def kernel(
    density_hbm,
    pattern_hbm,
    out_ref,
    density,
    pattern,
    kept,
    left,
    packed,
    incoming,
    total_low,
    total_high,
    ship,
    landed,
    load_sems,
    credits,
    left_sems,
    send_sems,
    recv_sems,
    ship_sems,
):
    rows, cols = lax.axis_size("row"), lax.axis_size("col")
    a, b, z = lax.axis_index("row"), lax.axis_index("col"), lax.axis_index("depth")
    other = 1 - z
    size = density.shape[-1]

    loads = [
        pltpu.make_async_copy(density_hbm.at[0], density, load_sems.at[0]),
        pltpu.make_async_copy(pattern_hbm, pattern, load_sems.at[1]),
    ]
    for load in loads:
        load.start()

    def place_of(t, layer):
        step_a, step_b = STEPS[t]
        return (
            lax.rem(a - step_a + rows, rows),
            lax.rem(b - step_b + cols, cols),
            layer,
        )

    def device(t, layer):
        return dict(zip(("row", "col", "depth"), place_of(t, layer)))

    def rank(place):
        index = (place[0] * cols + place[1]) * 2 + place[2]
        return jnp.where(index == 0, 8 * cols - 1, 2 * index)

    mine = rank((a, b, z))
    partners = [(t, layer) for t in AWAY for layer in range(2)] + [(CENTRE, other)]
    later = {}
    for t, layer in partners:
        later[t, 0 if t == CENTRE else layer] = rank(place_of(t, layer)) > mine

    def is_later(t, layer):
        return later[t, 0 if t == CENTRE else layer]

    def credit(t, layer):
        return credits.at[t, 0 if t == CENTRE else layer]

    barrier = pltpu.get_barrier_semaphore()
    earlier = jnp.int32(0)
    for t, layer in partners:
        earlier += jnp.where(is_later(t, layer), 0, 1)

        @pl.when(is_later(t, layer))
        def _(t=t, layer=layer):
            pl.semaphore_signal(
                barrier, inc=1, device_id=device(t, layer), device_id_type=MESH
            )

    @pl.when(earlier > 0)
    def _():
        pl.semaphore_wait(barrier, earlier)

    for t, layer in partners:

        @pl.when(jnp.logical_not(is_later(t, layer)))
        def _(t=t, layer=layer):
            pl.semaphore_signal(
                credits.at[8 - t, 0 if t == CENTRE else z],
                inc=1,
                device_id=device(t, layer),
                device_id_type=MESH,
            )

    def ready(t, layer):
        @pl.when(is_later(t, layer))
        def _():
            pl.semaphore_wait(credit(t, layer), 1)

    copies = []

    def copy_to(src, dst, send_sem, recv_sem, target):
        copy = pltpu.make_async_remote_copy(
            src_ref=src,
            dst_ref=dst,
            send_sem=send_sem,
            recv_sem=recv_sem,
            device_id=target,
            device_id_type=MESH,
        )
        copies.append(copy)
        return copy

    def send(t, layer):
        first, count = tiles_of(t)
        return copy_to(
            packed.at[layer, pl.ds(first, count)],
            incoming.at[t, z, pl.ds(0, count)],
            send_sems.at[t, 0 if t == CENTRE else layer],
            recv_sems.at[t, z],
            device(t, layer),
        )

    def keep(slots):
        for slot in slots:
            for layer in range(2):
                place = 3 * slot + 1 + layer - z
                block = density[place]
                kept[layer, slot] = jnp.where(
                    pattern[0, place] != 0, block, jnp.zeros_like(block)
                )

    def pack(tiles):
        for tile in tiles:
            for layer in range(2):
                packed[layer, tile] = jnp.concatenate(
                    [kept[layer, STEPS.index(step)] for step in TILES[tile]], axis=1
                )

    for load in loads:
        load.wait()
    keep(range(3, 9))
    pack(range(5, 8))

    up = [(t, layer, send(t, layer)) for t in ROW_UP for layer in range(2)]
    last_row = a == rows - 1

    def send_up():
        for t, layer, copy in up:
            ready(t, layer)
            copy.start()

    def sent_up():
        for _, _, copy in up:
            copy.wait_send()

    pl.when(last_row)(send_up)
    keep(range(3))
    pack(range(5))
    for slot in range(9):
        left[z, slot] = jnp.concatenate([kept[0, slot], kept[1, slot]], axis=1)
    pl.when(last_row)(sent_up)

    for layer in (1, 0):
        for t in COLUMN:
            ready(t, layer)
            send(t, layer).start()
    sibling = device(CENTRE, other)
    ready(CENTRE, other)
    copy_to(left.at[z], left.at[z], left_sems.at[0], left_sems.at[1], sibling).start()
    send(CENTRE, other).start()
    pl.when(jnp.logical_not(last_row))(send_up)

    down = [(t, layer, send(t, layer)) for layer in (1, 0) for t in ROW_DOWN]

    def send_down():
        for t, layer, copy in down:
            ready(t, layer)
            copy.start()

    pl.when(a > 0)(send_down)

    def arrived(ref, sem):
        pltpu.make_async_copy(ref, ref, sem).wait()

    def product(t):
        lhs = jnp.concatenate([left[0, t], left[1, t]], axis=0)
        tiles = [
            jnp.concatenate([incoming[t, 0, j], incoming[t, 1, j]], axis=0)
            for j in range(tiles_of(t)[1])
        ]
        found = jnp.dot(
            lhs, jnp.concatenate(tiles, axis=1), preferred_element_type=jnp.float32
        )
        return [
            found[:, 2 * size * j : 2 * size * (j + 1)].reshape(2, size, 2 * size)
            for j in range(len(tiles))
        ]

    def receive(t):
        for layer in range(2):
            arrived(incoming.at[t, layer, pl.ds(0, tiles_of(t)[1])], recv_sems.at[t, layer])

    nothing = jnp.zeros((size, size), out_ref.dtype)

    def put(goal_a, goal_b, layer, block):
        place = 3 * STEPS.index((goal_a, goal_b)) + 1 + layer - z
        out_ref[0, place] = jnp.where(pattern[0, place] != 0, block, nothing)

    for j in range(5):
        incoming[CENTRE, z, j] = packed[z, j]
    arrived(left.at[other], left_sems.at[1])
    arrived(incoming.at[CENTRE, other], recv_sems.at[CENTRE, other])
    parts = product(CENTRE)
    blank = jnp.zeros((2, size, size), jnp.float32)
    for sb in range(3):
        total_low[sb] = parts[1 + sb]
    total_high[0] = jnp.concatenate([blank, parts[0][:, :, :size]], axis=2)
    total_high[1] = jnp.concatenate([blank, parts[0][:, :, size:]], axis=2)
    total_high[2] = jnp.concatenate([blank, parts[4][:, :, size:]], axis=2)
    for t in COLUMN:
        receive(t)
        parts = product(t)
        if t == 3:
            low, pair, at = parts[:2], parts[2], 0
        else:
            low, pair, at = parts[1:], parts[0], 1
        for i in range(2):
            total_low[at + i] += low[i]
        total_high[at] += jnp.concatenate([blank, pair[:, :, :size]], axis=2)
        total_high[at + 1] += jnp.concatenate([blank, pair[:, :, size:]], axis=2)

    def row_part(t, total):
        parts = product(t)
        at = {-1: 0, 0: 0, 1: 1}[STEPS[t][1]]
        for i, part in enumerate(parts):
            total[at + i] += part

    for t in ROW_DOWN:
        receive(t)
        row_part(t, total_high)
    for sb in range(3):
        total_low[sb] += jnp.concatenate([blank, total_high[sb][:, :, :size]], axis=2)
        ship[0, sb] = total_high[sb, other].astype(ship.dtype)

    copy_to(ship.at[0], landed.at[0], ship_sems.at[0, 0], ship_sems.at[0, 1], sibling).start()
    pl.when(a == 0)(send_down)

    for target in range(9):
        out_ref[0, 3 * target + 1 + z - other] = nothing
    for sb in range(3):
        own = total_high[sb, z].astype(out_ref.dtype)
        put(1, sb - 1, z, own[:, size:])
    arrived(landed.at[0], ship_sems.at[0, 1])
    for sb in range(3):
        put(1, sb - 1, other, landed[0, sb][:, size:])

    for t in ROW_UP:
        receive(t)
        row_part(t, total_low)
    for sb in range(3):
        ship[1, sb] = total_low[sb, other].astype(ship.dtype)
    copy_to(ship.at[1], landed.at[1], ship_sems.at[1, 0], ship_sems.at[1, 1], sibling).start()
    for sb in range(3):
        own = total_low[sb, z].astype(out_ref.dtype)
        put(-1, sb - 1, z, own[:, :size])
        put(0, sb - 1, z, own[:, size:])
    pl.when(jnp.logical_not(last_row))(sent_up)
    for copy in copies[len(up) : -1]:
        copy.wait_send()
    arrived(landed.at[1], ship_sems.at[1, 1])
    for sb in range(3):
        put(-1, sb - 1, other, landed[1, sb][:, :size])
        put(0, sb - 1, other, landed[1, sb][:, size:])
    copies[-1].wait_send()


def local(density, pattern):
    size = density.shape[-1]
    kind = density.dtype
    wide = 2 * size
    return pl.pallas_call(
        kernel,
        out_shape=jax.ShapeDtypeStruct(density.shape, kind),
        in_specs=[pl.BlockSpec(memory_space=pltpu.HBM)] * 2,
        out_specs=pl.BlockSpec(memory_space=pltpu.VMEM),
        scratch_shapes=[
            pltpu.VMEM((27, size, size), kind),
            pltpu.SMEM(pattern.shape, pattern.dtype),
            pltpu.VMEM((2, 9, size, size), kind),
            pltpu.VMEM((2, 9, size, wide), kind),
            pltpu.VMEM((2, len(TILES), size, wide), kind),
            pltpu.VMEM((9, 2, 5, size, wide), kind),
            pltpu.VMEM((3, 2, size, wide), jnp.float32),
            pltpu.VMEM((3, 2, size, wide), jnp.float32),
            pltpu.VMEM((2, 3, size, wide), kind),
            pltpu.VMEM((2, 3, size, wide), kind),
            pltpu.SemaphoreType.DMA((2,)),
            pltpu.SemaphoreType.REGULAR((9, 2)),
            pltpu.SemaphoreType.DMA((2,)),
            pltpu.SemaphoreType.DMA((9, 2)),
            pltpu.SemaphoreType.DMA((9, 2)),
            pltpu.SemaphoreType.DMA((2, 2)),
        ],
        compiler_params=pltpu.CompilerParams(
            collective_id=0,
            has_side_effects=True,
            vmem_limit_bytes=32 * 1024 * 1024,
        ),
    )(
        pltpu.with_memory_space_constraint(density, pltpu.HBM),
        pltpu.with_memory_space_constraint(pattern, pltpu.HBM),
    )


def solution(mesh):
    placed = (P(("row", "col", "depth"), None, None, None), P(("row", "col", "depth"), None))
    return jax.shard_map(
        local,
        mesh=mesh,
        in_specs=placed,
        out_specs=P(("row", "col", "depth"), None, None, None),
        check_vma=False,
    )
```

```python
import jax
import jax.numpy as jnp
from jax import lax
from jax.experimental import pallas as pl
from jax.experimental.pallas import tpu as pltpu
from jax.sharding import PartitionSpec as P

MESH = pl.DeviceIdType.MESH
STEPS = [(a, b) for a in (-1, 0, 1) for b in (-1, 0, 1)]
CENTRE = 4
ROW_UP = [0, 2, 1]
COLUMN = [3, 5]
ROW_DOWN = [7]
SENT = ROW_UP + COLUMN + ROW_DOWN + [CENTRE]
AWAY = [0, 1, 2, 3, 5, 6, 7, 8]

TILES = [
    ((1, -1), (1, 0)),
    ((-1, -1), (0, -1)),
    ((-1, 0), (0, 0)),
    ((-1, 1), (0, 1)),
    ((1, 0), (1, 1)),
    ((0, -1), (1, -1)),
    ((0, 0), (1, 0)),
    ((0, 1), (1, 1)),
]


def tiles_of(t):
    a, b = STEPS[t]
    if a == 0:
        return {-1: (2, 3), 0: (0, 5), 1: (0, 3)}[b]
    first = 5 if a == -1 else 1
    return {-1: (first + 1, 2), 0: (first, 3), 1: (first, 2)}[b]


def kernel(
    density_hbm,
    pattern_hbm,
    out_ref,
    density,
    pattern,
    kept,
    left,
    packed,
    incoming,
    total_low,
    total_high,
    ship,
    landed,
    load_sems,
    credits,
    relay,
    left_sems,
    send_sems,
    recv_sems,
    ship_sems,
):
    rows, cols = lax.axis_size("row"), lax.axis_size("col")
    a, b, z = lax.axis_index("row"), lax.axis_index("col"), lax.axis_index("depth")
    other = 1 - z
    size = density.shape[-1]

    def load(first, count, sem):
        return pltpu.make_async_copy(
            density_hbm.at[0, pl.ds(first, count), pl.ds(1 - z, 2)],
            density.at[pl.ds(first, count)],
            load_sems.at[sem],
        )

    load_pattern = pltpu.make_async_copy(pattern_hbm, pattern, load_sems.at[0])
    load_first, load_rest = load(3, 6, 1), load(0, 3, 2)
    for copy in (load_pattern, load_first, load_rest):
        copy.start()

    def place_of(t, layer):
        step_a, step_b = STEPS[t]
        return (
            lax.rem(a - step_a + rows, rows),
            lax.rem(b - step_b + cols, cols),
            layer,
        )

    def device(t, layer):
        return dict(zip(("row", "col", "depth"), place_of(t, layer)))

    def rank(place):
        row, col, layer = place
        inside = col * 2 + layer
        index = row * 2 * cols + inside
        late = jnp.where(row == rows - 1, 4 * cols + 1 + inside, 8 * cols + index)
        return jnp.where(index == 0, 4 * cols, jnp.where(row < 2, index, late))

    last_row = a == rows - 1
    mine = rank((a, b, z))
    partners = [(t, layer) for t in AWAY for layer in range(2)] + [(CENTRE, other)]
    direct = jnp.logical_not(last_row)
    later, before = {}, {}
    for t, layer in partners:
        key = t, 0 if t == CENTRE else layer
        after = rank(place_of(t, layer)) > mine
        later[key], before[key] = after, jnp.logical_not(after)
        if STEPS[t][0] == 0:
            later[key] = jnp.logical_and(direct, after)
            before[key] = jnp.logical_and(direct, jnp.logical_not(after))

    def is_later(t, layer):
        return later[t, 0 if t == CENTRE else layer]

    def is_earlier(t, layer):
        return before[t, 0 if t == CENTRE else layer]

    def credit(t, layer):
        return credits.at[t, 0 if t == CENTRE else layer]

    barrier = pltpu.get_barrier_semaphore()
    earlier = jnp.int32(0)
    for t, layer in partners:
        earlier += jnp.where(is_earlier(t, layer), 1, 0)

        @pl.when(is_later(t, layer))
        def _(t=t, layer=layer):
            pl.semaphore_signal(
                barrier, inc=1, device_id=device(t, layer), device_id_type=MESH
            )

    @pl.when(earlier > 0)
    def _():
        pl.semaphore_wait(barrier, earlier)

    def enter():
        for t in ROW_UP:
            for layer in range(2):
                pl.semaphore_signal(
                    relay.at[0], inc=1, device_id=device(t, layer), device_id_type=MESH
                )

    pl.when(last_row)(enter)
    for t, layer in partners:
        if 8 - t not in SENT:
            continue
        credited = is_earlier(t, layer)
        if t in ROW_UP:
            credited = jnp.logical_and(direct, credited)

        @pl.when(credited)
        def _(t=t, layer=layer):
            pl.semaphore_signal(
                credits.at[8 - t, 0 if t == CENTRE else z],
                inc=1,
                device_id=device(t, layer),
                device_id_type=MESH,
            )

    def ready(t, layer):
        @pl.when(is_later(t, layer))
        def _():
            pl.semaphore_wait(credit(t, layer), 1)

    copies = []

    def copy_to(src, dst, send_sem, recv_sem, target):
        copy = pltpu.make_async_remote_copy(
            src_ref=src,
            dst_ref=dst,
            send_sem=send_sem,
            recv_sem=recv_sem,
            device_id=target,
            device_id_type=MESH,
        )
        copies.append(copy)
        return copy

    def send(t, layer):
        first, count = tiles_of(t)
        return copy_to(
            packed.at[layer, pl.ds(first, count)],
            incoming.at[t, z, pl.ds(0, count)],
            send_sems.at[t, 0 if t == CENTRE else layer],
            recv_sems.at[t, z],
            device(t, layer),
        )

    def keep(slots):
        for slot in slots:
            for layer in range(2):
                place = 3 * slot + 1 + layer - z
                block = density[slot, layer]
                kept[layer, slot] = jnp.where(
                    pattern[0, place] != 0, block, jnp.zeros_like(block)
                )

    def pack(tiles):
        for tile in tiles:
            for layer in range(2):
                packed[layer, tile] = jnp.concatenate(
                    [kept[layer, STEPS.index(step)] for step in TILES[tile]], axis=1
                )

    load_pattern.wait()
    load_first.wait()
    keep(range(3, 9))
    pack(range(5, 8))

    up = [(t, layer, send(t, layer)) for t in ROW_UP for layer in range(2)]

    def send_up():
        for t, layer, copy in up:
            ready(t, layer)
            copy.start()

    def sent_up():
        for _, _, copy in up:
            copy.wait_send()

    pl.when(last_row)(send_up)
    load_rest.wait()
    keep(range(3))
    pack(range(5))
    for slot in range(9):
        left[z, slot] = jnp.concatenate([kept[0, slot], kept[1, slot]], axis=1)

    @pl.when(last_row)
    def _():
        sent_up()
        pl.semaphore_wait(relay.at[1], 1)

    def send_columns(layer):
        for t in COLUMN:
            ready(t, layer)
            send(t, layer).start()

    send_columns(1)
    pl.when(jnp.logical_not(last_row))(send_up)
    sibling = device(CENTRE, other)
    ready(CENTRE, other)
    copy_to(left.at[z], left.at[z], left_sems.at[0], left_sems.at[1], sibling).start()
    send(CENTRE, other).start()
    send_columns(0)

    down = [(t, layer, send(t, layer)) for layer in (1, 0) for t in ROW_DOWN]

    @pl.when(a > 0)
    def _():
        for t, layer, copy in down:
            ready(t, layer)
            copy.start()

    def arrived(ref, sem):
        pltpu.make_async_copy(ref, ref, sem).wait()

    def product(t):
        lhs = jnp.concatenate([left[0, t], left[1, t]], axis=0)
        tiles = [
            jnp.concatenate([incoming[t, 0, j], incoming[t, 1, j]], axis=0)
            for j in range(tiles_of(t)[1])
        ]
        found = jnp.dot(
            lhs, jnp.concatenate(tiles, axis=1), preferred_element_type=jnp.float32
        )
        return [
            found[:, 2 * size * j : 2 * size * (j + 1)].reshape(2, size, 2 * size)
            for j in range(len(tiles))
        ]

    def receive(t):
        for layer in range(2):
            arrived(incoming.at[t, layer, pl.ds(0, tiles_of(t)[1])], recv_sems.at[t, layer])

    nothing = jnp.zeros((size, size), out_ref.dtype)

    def put(goal_a, goal_b, layer, block):
        place = 3 * STEPS.index((goal_a, goal_b)) + 1 + layer - z
        out_ref[0, place] = jnp.where(pattern[0, place] != 0, block, nothing)

    receive(7)
    for corner, column, first in ((6, 3, 1), (8, 5, 0)):
        for layer in range(2):
            copy_to(
                incoming.at[7, layer, pl.ds(first, 2)],
                incoming.at[corner, layer, pl.ds(0, 2)],
                send_sems.at[corner, layer],
                recv_sems.at[corner, layer],
                device(column, z),
            ).start()

    for j in range(5):
        incoming[CENTRE, z, j] = packed[z, j]
    arrived(left.at[other], left_sems.at[1])
    arrived(incoming.at[CENTRE, other], recv_sems.at[CENTRE, other])
    parts = product(CENTRE)
    blank = jnp.zeros((2, size, size), jnp.float32)
    for sb in range(3):
        total_low[sb] = parts[1 + sb]
    total_high[0] = jnp.concatenate([blank, parts[0][:, :, :size]], axis=2)
    total_high[1] = jnp.concatenate([blank, parts[0][:, :, size:]], axis=2)
    total_high[2] = jnp.concatenate([blank, parts[4][:, :, size:]], axis=2)
    for t in COLUMN:
        receive(t)
        parts = product(t)
        if t == 3:
            low, pair, at = parts[:2], parts[2], 0
        else:
            low, pair, at = parts[1:], parts[0], 1
        for i in range(2):
            total_low[at + i] += low[i]
        total_high[at] += jnp.concatenate([blank, pair[:, :, :size]], axis=2)
        total_high[at + 1] += jnp.concatenate([blank, pair[:, :, size:]], axis=2)

    def row_part(t, total):
        parts = product(t)
        at = {-1: 0, 0: 0, 1: 1}[STEPS[t][1]]
        for i, part in enumerate(parts):
            total[at + i] += part

    row_part(7, total_high)
    for t in (6, 8):
        receive(t)
        row_part(t, total_high)
    for sb in range(3):
        total_low[sb] += jnp.concatenate([blank, total_high[sb][:, :, :size]], axis=2)
        ship[0, sb] = total_high[sb, other].astype(ship.dtype)

    copy_to(ship.at[0], landed.at[0], ship_sems.at[0, 0], ship_sems.at[0, 1], sibling).start()

    @pl.when(a == 0)
    def _():
        pl.semaphore_wait(relay.at[0], 6)
        pl.semaphore_signal(
            relay.at[1], inc=1, device_id=device(7, z), device_id_type=MESH
        )
        for _, _, copy in down:
            copy.start()

    for target in range(9):
        out_ref[0, 3 * target + 1 + z - other] = nothing
    for sb in range(3):
        own = total_high[sb, z].astype(out_ref.dtype)
        put(1, sb - 1, z, own[:, size:])
    arrived(landed.at[0], ship_sems.at[0, 1])
    for sb in range(3):
        put(1, sb - 1, other, landed[0, sb][:, size:])

    for t in ROW_UP:
        receive(t)
        row_part(t, total_low)
    for sb in range(3):
        ship[1, sb] = total_low[sb, other].astype(ship.dtype)
    copy_to(ship.at[1], landed.at[1], ship_sems.at[1, 0], ship_sems.at[1, 1], sibling).start()
    for sb in range(3):
        own = total_low[sb, z].astype(out_ref.dtype)
        put(-1, sb - 1, z, own[:, :size])
        put(0, sb - 1, z, own[:, size:])
    pl.when(jnp.logical_not(last_row))(sent_up)
    for copy in copies[len(up) : -1]:
        copy.wait_send()
    arrived(landed.at[1], ship_sems.at[1, 1])
    for sb in range(3):
        put(-1, sb - 1, other, landed[1, sb][:, :size])
        put(0, sb - 1, other, landed[1, sb][:, size:])
    copies[-1].wait_send()


def local(density, pattern):
    size = density.shape[-1]
    kind = density.dtype
    wide = 2 * size
    return pl.pallas_call(
        kernel,
        out_shape=jax.ShapeDtypeStruct(density.shape, kind),
        in_specs=[pl.BlockSpec(memory_space=pltpu.HBM)] * 2,
        out_specs=pl.BlockSpec(memory_space=pltpu.VMEM),
        scratch_shapes=[
            pltpu.VMEM((9, 2, size, size), kind),
            pltpu.SMEM(pattern.shape, pattern.dtype),
            pltpu.VMEM((2, 9, size, size), kind),
            pltpu.VMEM((2, 9, size, wide), kind),
            pltpu.VMEM((2, len(TILES), size, wide), kind),
            pltpu.VMEM((9, 2, 5, size, wide), kind),
            pltpu.VMEM((3, 2, size, wide), jnp.float32),
            pltpu.VMEM((3, 2, size, wide), jnp.float32),
            pltpu.VMEM((2, 3, size, wide), kind),
            pltpu.VMEM((2, 3, size, wide), kind),
            pltpu.SemaphoreType.DMA((3,)),
            pltpu.SemaphoreType.REGULAR((9, 2)),
            pltpu.SemaphoreType.REGULAR((2,)),
            pltpu.SemaphoreType.DMA((2,)),
            pltpu.SemaphoreType.DMA((9, 2)),
            pltpu.SemaphoreType.DMA((9, 2)),
            pltpu.SemaphoreType.DMA((2, 2)),
        ],
        compiler_params=pltpu.CompilerParams(
            collective_id=0,
            has_side_effects=True,
            vmem_limit_bytes=32 * 1024 * 1024,
        ),
    )(
        pltpu.with_memory_space_constraint(
            density.reshape(1, 9, 3, size, size), pltpu.HBM
        ),
        pltpu.with_memory_space_constraint(pattern, pltpu.HBM),
    )


def solution(mesh):
    placed = (P(("row", "col", "depth"), None, None, None), P(("row", "col", "depth"), None))
    return jax.shard_map(
        local,
        mesh=mesh,
        in_specs=placed,
        out_specs=P(("row", "col", "depth"), None, None, None),
        check_vma=False,
    )
```

```python
import jax
import jax.numpy as jnp
from jax import lax
from jax.experimental import pallas as pl
from jax.experimental.pallas import tpu as pltpu
from jax.sharding import PartitionSpec as P

MESH = pl.DeviceIdType.MESH
STEPS = [(a, b) for a in (-1, 0, 1) for b in (-1, 0, 1)]
CENTRE = 4
ROW_UP = [0, 2, 1]
COLUMN = [3, 5]
ROW_DOWN = [7]
SENT = ROW_UP + COLUMN + ROW_DOWN + [CENTRE]
AWAY = [0, 1, 2, 3, 5, 6, 7, 8]

TILES = [
    ((1, -1), (1, 0)),
    ((-1, -1), (0, -1)),
    ((-1, 0), (0, 0)),
    ((-1, 1), (0, 1)),
    ((1, 0), (1, 1)),
    ((0, -1), (1, -1)),
    ((0, 0), (1, 0)),
    ((0, 1), (1, 1)),
]


def tiles_of(t):
    a, b = STEPS[t]
    if a == 0:
        return {-1: (2, 3), 0: (0, 5), 1: (0, 3)}[b]
    first = 5 if a == -1 else 1
    return {-1: (first + 1, 2), 0: (first, 3), 1: (first, 2)}[b]


def kernel(
    density_hbm,
    pattern_hbm,
    out_ref,
    density,
    pattern,
    kept,
    left,
    packed,
    incoming,
    total_low,
    total_high,
    ship,
    landed,
    load_sems,
    credits,
    relay,
    extra,
    staged,
    partly,
    extra_sems,
    part_sems,
    pass_sems,
    left_sems,
    send_sems,
    recv_sems,
    ship_sems,
):
    rows, cols = lax.axis_size("row"), lax.axis_size("col")
    a, b, z = lax.axis_index("row"), lax.axis_index("col"), lax.axis_index("depth")
    other = 1 - z
    size = density.shape[-1]

    def load(first, count, sem):
        return pltpu.make_async_copy(
            density_hbm.at[0, pl.ds(first, count), pl.ds(1 - z, 2)],
            density.at[pl.ds(first, count)],
            load_sems.at[sem],
        )

    load_pattern = pltpu.make_async_copy(pattern_hbm, pattern, load_sems.at[0])
    load_first, load_rest = [load(4, 2, 1), load(7, 2, 2)], [load(3, 1, 3), load(6, 1, 4), load(0, 3, 5)]
    for copy in [load_pattern] + load_first + load_rest:
        copy.start()

    last, end = rows - 1, cols - 1
    last_row, first_row = a == last, a == 0
    meeting = first_row & (b == 0)
    row_of = {-1: jnp.where(last_row, 0, a + 1), 0: a, 1: jnp.where(first_row, last, a - 1)}
    col_of = {-1: jnp.where(b == end, 0, b + 1), 0: b, 1: jnp.where(b == 0, end, b - 1)}

    def device(t, layer):
        step_a, step_b = STEPS[t]
        return {"row": row_of[step_a], "col": col_of[step_b], "depth": layer}

    partners = [(t, layer) for t in AWAY for layer in range(2)] + [(CENTRE, other)]
    direct = jnp.logical_not(last_row)
    is_first = first_row & (b == 0) & (z == 0)
    row_later = {
        -1: direct & (a != last - 1 if rows > 3 else a < last) & jnp.logical_not(is_first),
        1: first_row | last_row if rows > 3 else first_row,
    }
    col_later = {-1: b != end, 0: z == 0, 1: b == 0}
    later, before, late = {}, {}, {}
    for t, layer in partners:
        step_a, step_b = STEPS[t]
        key = t, 0 if t == CENTRE else layer
        to_first = jnp.bool_(False)
        if step_a == 1 or step_a == 0:
            to_first = (row_of[step_a] == 0) & (col_of[step_b] == 0)
            to_first = to_first & (layer == 0)
        if step_a == 0:
            after = direct & ((col_later[step_b] & jnp.logical_not(is_first)) | to_first)
            ahead = direct & jnp.logical_not(after)
        else:
            after = row_later[step_a] | to_first
            ahead = jnp.logical_not(after)
        later[key], before[key], late[key] = after, ahead, to_first

    def is_later(t, layer):
        return later[t, 0 if t == CENTRE else layer]

    def is_earlier(t, layer):
        return before[t, 0 if t == CENTRE else layer]

    def credit(t, layer):
        return credits.at[t, 0 if t == CENTRE else layer]

    barrier = pltpu.get_barrier_semaphore()

    def greet():
        for t, layer in partners:

            @pl.when(is_later(t, layer))
            def _(t=t, layer=layer):
                pl.semaphore_signal(
                    barrier, inc=1, device_id=device(t, layer), device_id_type=MESH
                )

    def meet():
        earlier = jnp.int32(0)
        for t, layer in partners:
            earlier += is_earlier(t, layer).astype(jnp.int32)

        @pl.when(earlier > 0)
        def _():
            pl.semaphore_wait(barrier, earlier)

    @pl.when(direct)
    def _():
        greet()
        meet()
        for t, layer in partners:
            if 8 - t not in SENT:
                continue

            @pl.when(is_earlier(t, layer))
            def _(t=t, layer=layer):
                pl.semaphore_signal(
                    credits.at[8 - t, 0 if t == CENTRE else z],
                    inc=1,
                    device_id=device(t, layer),
                    device_id_type=MESH,
                )

    @pl.when(last_row)
    def _():
        meet()
        for t in ROW_UP:
            for layer in range(2):
                pl.semaphore_signal(
                    relay.at[0 if t == 1 else 1],
                    inc=1,
                    device_id=device(t, layer),
                    device_id_type=MESH,
                )

    def ready(t, layer):
        @pl.when(is_later(t, layer))
        def _():
            pl.semaphore_wait(credit(t, layer), 1)

    copies = []

    def copy_to(src, dst, send_sem, recv_sem, target):
        copy = pltpu.make_async_remote_copy(
            src_ref=src,
            dst_ref=dst,
            send_sem=send_sem,
            recv_sem=recv_sem,
            device_id=target,
            device_id_type=MESH,
        )
        copies.append(copy)
        return copy

    def send(t, layer):
        first, count = tiles_of(t)
        return copy_to(
            packed.at[layer, pl.ds(first, count)],
            incoming.at[t, z, pl.ds(0, count)],
            send_sems.at[t, 0 if t == CENTRE else layer],
            recv_sems.at[t, z],
            device(t, layer),
        )

    def keep(slots):
        for slot in slots:
            for layer in range(2):
                place = 3 * slot + 1 + layer - z
                block = density[slot, layer]
                kept[layer, slot] = jnp.where(
                    pattern[0, place] != 0, block, jnp.zeros_like(block)
                )

    def pack(tiles):
        for tile in tiles:
            for layer in range(2):
                packed[layer, tile] = jnp.concatenate(
                    [kept[layer, STEPS.index(step)] for step in TILES[tile]], axis=1
                )

    load_pattern.wait()
    for copy in load_first:
        copy.wait()
    keep((4, 5, 7, 8))
    pack((6, 7))

    up = [(t, layer, send(t, layer)) for t in ROW_UP for layer in (1, 0)]
    around = [
        copy_to(
            packed.at[1 - layer, pl.ds(6, 2)],
            extra.at[z],
            pass_sems.at[layer],
            extra_sems.at[z],
            device(0, layer),
        )
        for layer in range(2)
    ]
    far = last_row & (b == end)

    def send_up(messages=up):
        for t, layer, copy in messages:
            ready(t, layer)
            copy.start()
            if t == 0:
                pl.when(far)(around[layer].start)

    def sent_up():
        for _, _, copy in up:
            copy.wait_send()

        @pl.when(far)
        def _():
            for copy in around:
                copy.wait_send()

    pl.when(last_row)(lambda: send_up(up[:2]))
    for copy in load_rest:
        copy.wait()
    keep((3, 6))
    pack((5,))

    @pl.when(last_row)
    def _():
        send_up(up[2:])
        greet()

    keep(range(3))
    pack(range(5))
    for slot in range(9):
        left[z, slot] = jnp.concatenate([kept[0, slot], kept[1, slot]], axis=1)

    @pl.when(last_row)
    def _():
        sent_up()
        pl.semaphore_wait(relay.at[2], 1)

    sibling = device(CENTRE, other)
    swap = copy_to(left.at[z], left.at[z], left_sems.at[0], left_sems.at[1], sibling)
    near = [(t, layer, [send(t, layer)]) for t in COLUMN for layer in range(2)]
    near.append((CENTRE, other, [swap, send(CENTRE, other)]))
    down = [(t, layer, send(t, layer)) for t in ROW_DOWN for layer in range(2)]

    def offer(messages, wanted):
        for t, layer, group in messages:

            @pl.when(wanted(t, layer))
            def _(t=t, layer=layer, group=group):
                ready(t, layer)
                for copy in group:
                    copy.start()

    def to_first(t, layer):
        return late[t, 0 if t == CENTRE else layer]

    downward = [(t, layer, [copy]) for t, layer, copy in down]
    offer(near, lambda t, layer: jnp.logical_not(to_first(t, layer)))
    offer(downward, lambda t, layer: (a > 0) & jnp.logical_not(to_first(t, layer)))
    pl.when(direct)(send_up)
    offer([m for m in near if m[0] == CENTRE or m[1] == 0], to_first)
    offer(downward[:1], lambda t, layer: (a > 0) & to_first(t, layer))

    def arrived(ref, sem):
        pltpu.make_async_copy(ref, ref, sem).wait()

    def product(t):
        lhs = jnp.concatenate([left[0, t], left[1, t]], axis=0)
        tiles = [
            jnp.concatenate([incoming[t, 0, j], incoming[t, 1, j]], axis=0)
            for j in range(tiles_of(t)[1])
        ]
        found = jnp.dot(
            lhs, jnp.concatenate(tiles, axis=1), preferred_element_type=jnp.float32
        )
        return [
            found[:, 2 * size * j : 2 * size * (j + 1)].reshape(2, size, 2 * size)
            for j in range(len(tiles))
        ]

    def receive(t):
        for layer in range(2):
            arrived(incoming.at[t, layer, pl.ds(0, tiles_of(t)[1])], recv_sems.at[t, layer])

    nothing = jnp.zeros((size, size), out_ref.dtype)

    def put(goal_a, goal_b, layer, block):
        place = 3 * STEPS.index((goal_a, goal_b)) + 1 + layer - z
        out_ref[0, place] = jnp.where(pattern[0, place] != 0, block, nothing)

    receive(7)
    for corner, column, first in ((6, 3, 1), (8, 5, 0)):
        for layer in range(2):
            copy_to(
                incoming.at[7, layer, pl.ds(first, 2)],
                incoming.at[corner, layer, pl.ds(0, 2)],
                send_sems.at[corner, layer],
                recv_sems.at[corner, layer],
                device(column, z),
            ).start()

    for j in range(5):
        incoming[CENTRE, z, j] = packed[z, j]
    arrived(left.at[other], left_sems.at[1])
    arrived(incoming.at[CENTRE, other], recv_sems.at[CENTRE, other])
    parts = product(CENTRE)
    blank = jnp.zeros((2, size, size), jnp.float32)
    for sb in range(3):
        total_low[sb] = parts[1 + sb]
    total_high[0] = jnp.concatenate([blank, parts[0][:, :, :size]], axis=2)
    total_high[1] = jnp.concatenate([blank, parts[0][:, :, size:]], axis=2)
    total_high[2] = jnp.concatenate([blank, parts[4][:, :, size:]], axis=2)
    for t in COLUMN:
        receive(t)
        parts = product(t)
        if t == 3:
            low, pair, at = parts[:2], parts[2], 0
        else:
            low, pair, at = parts[1:], parts[0], 1
        for i in range(2):
            total_low[at + i] += low[i]
        total_high[at] += jnp.concatenate([blank, pair[:, :, :size]], axis=2)
        total_high[at + 1] += jnp.concatenate([blank, pair[:, :, size:]], axis=2)

    def row_part(t, total):
        parts = product(t)
        at = {-1: 0, 0: 0, 1: 1}[STEPS[t][1]]
        for i, part in enumerate(parts):
            total[at + i] += part

    row_part(7, total_high)
    for t in (6, 8):
        receive(t)
        row_part(t, total_high)
    for sb in range(3):
        total_low[sb] += jnp.concatenate([blank, total_high[sb][:, :, :size]], axis=2)
        ship[0, sb] = total_high[sb, other].astype(ship.dtype)

    copy_to(ship.at[0], landed.at[0], ship_sems.at[0, 0], ship_sems.at[0, 1], sibling).start()

    @pl.when(a == 0)
    def _():
        pl.semaphore_wait(relay.at[0], 2)
        for _, _, copy in down:
            copy.start()

    for target in range(9):
        out_ref[0, 3 * target + 1 + z - other] = nothing
    for sb in range(3):
        own = total_high[sb, z].astype(out_ref.dtype)
        put(1, sb - 1, z, own[:, size:])

    sent = copies[len(up) + len(around) :]

    def take(t):
        receive(t)
        row_part(t, total_low)

    @pl.when(first_row)
    def _():
        pl.semaphore_wait(relay.at[1], 4)
        pl.semaphore_signal(
            relay.at[2], inc=1, device_id=device(7, z), device_id_type=MESH
        )

    pl.when(jnp.logical_not(meeting))(lambda: take(0))
    take(2)
    take(1)
    partial = copy_to(staged, partly, part_sems.at[0], part_sems.at[1], sibling)
    swap_last = copy_to(
        ship.at[1], landed.at[1], ship_sems.at[1, 0], ship_sems.at[1, 1], sibling
    )

    @pl.when(meeting)
    def _():
        for sb in range(3):
            staged[sb] = total_low[sb, other]
        partial.start()
        arrived(partly, part_sems.at[1])
        for layer in range(2):
            arrived(extra.at[layer], extra_sems.at[layer])
        found = jnp.dot(
            left[z, 0],
            jnp.concatenate(
                [jnp.concatenate([extra[0, j], extra[1, j]], axis=0) for j in range(2)], axis=1
            ),
            preferred_element_type=jnp.float32,
        )
        for sb in range(3):
            whole = partly[sb]
            if sb < 2:
                whole += found[:, 2 * size * sb : 2 * size * (sb + 1)]
            landed[1, sb] = whole.astype(landed.dtype)
        take(0)

    for sb in range(3):
        ship[1, sb] = total_low[sb, other].astype(ship.dtype)

    pl.when(jnp.logical_not(meeting))(swap_last.start)
    arrived(landed.at[0], ship_sems.at[0, 1])
    for sb in range(3):
        put(1, sb - 1, other, landed[0, sb][:, size:])

    for sb in range(3):
        own = total_low[sb, z].astype(out_ref.dtype)
        put(-1, sb - 1, z, own[:, :size])
        put(0, sb - 1, z, own[:, size:])
    pl.when(jnp.logical_not(last_row))(sent_up)
    for copy in sent:
        copy.wait_send()

    pl.when(meeting)(partial.wait_send)
    pl.when(jnp.logical_not(meeting))(lambda: arrived(landed.at[1], ship_sems.at[1, 1]))
    for sb in range(3):
        put(-1, sb - 1, other, landed[1, sb][:, :size])
        put(0, sb - 1, other, landed[1, sb][:, size:])
    pl.when(jnp.logical_not(meeting))(swap_last.wait_send)


def local(density, pattern):
    size = density.shape[-1]
    kind = density.dtype
    wide = 2 * size
    return pl.pallas_call(
        kernel,
        out_shape=jax.ShapeDtypeStruct(density.shape, kind),
        in_specs=[pl.BlockSpec(memory_space=pltpu.HBM)] * 2,
        out_specs=pl.BlockSpec(memory_space=pltpu.VMEM),
        scratch_shapes=[
            pltpu.VMEM((9, 2, size, size), kind),
            pltpu.SMEM(pattern.shape, pattern.dtype),
            pltpu.VMEM((2, 9, size, size), kind),
            pltpu.VMEM((2, 9, size, wide), kind),
            pltpu.VMEM((2, len(TILES), size, wide), kind),
            pltpu.VMEM((9, 2, 5, size, wide), kind),
            pltpu.VMEM((3, 2, size, wide), jnp.float32),
            pltpu.VMEM((3, 2, size, wide), jnp.float32),
            pltpu.VMEM((2, 3, size, wide), kind),
            pltpu.VMEM((2, 3, size, wide), kind),
            pltpu.SemaphoreType.DMA((6,)),
            pltpu.SemaphoreType.REGULAR((9, 2)),
            pltpu.SemaphoreType.REGULAR((3,)),
            pltpu.VMEM((2, 2, size, wide), kind),
            pltpu.VMEM((3, size, wide), jnp.float32),
            pltpu.VMEM((3, size, wide), jnp.float32),
            pltpu.SemaphoreType.DMA((2,)),
            pltpu.SemaphoreType.DMA((2,)),
            pltpu.SemaphoreType.DMA((2,)),
            pltpu.SemaphoreType.DMA((2,)),
            pltpu.SemaphoreType.DMA((9, 2)),
            pltpu.SemaphoreType.DMA((9, 2)),
            pltpu.SemaphoreType.DMA((2, 2)),
        ],
        compiler_params=pltpu.CompilerParams(
            collective_id=0,
            has_side_effects=True,
            vmem_limit_bytes=32 * 1024 * 1024,
        ),
    )(
        pltpu.with_memory_space_constraint(
            density.reshape(1, 9, 3, size, size), pltpu.HBM
        ),
        pltpu.with_memory_space_constraint(pattern, pltpu.HBM),
    )


def solution(mesh):
    placed = (P(("row", "col", "depth"), None, None, None), P(("row", "col", "depth"), None))
    return jax.shard_map(
        local,
        mesh=mesh,
        in_specs=placed,
        out_specs=P(("row", "col", "depth"), None, None, None),
        check_vma=False,
    )
```

```python
import jax
import jax.numpy as jnp
from jax import lax
from jax.experimental import pallas as pl
from jax.experimental.pallas import tpu as pltpu
from jax.sharding import PartitionSpec as P

MESH = pl.DeviceIdType.MESH
STEPS = [(a, b) for a in (-1, 0, 1) for b in (-1, 0, 1)]
CENTRE = 4
ROW_UP = [0, 2, 1]
COLUMN = [3, 5]
ROW_DOWN = [7]
SENT = ROW_UP + COLUMN + ROW_DOWN + [CENTRE]
AWAY = [0, 1, 2, 3, 5, 6, 7, 8]

TILES = [
    ((1, -1), (1, 0)),
    ((-1, -1), (0, -1)),
    ((-1, 0), (0, 0)),
    ((-1, 1), (0, 1)),
    ((1, 0), (1, 1)),
    ((0, -1), (1, -1)),
    ((0, 0), (1, 0)),
    ((0, 1), (1, 1)),
]


def tiles_of(t):
    a, b = STEPS[t]
    if a == 0:
        return {-1: (2, 3), 0: (0, 5), 1: (0, 3)}[b]
    first = 5 if a == -1 else 1
    return {-1: (first + 1, 2), 0: (first, 3), 1: (first, 2)}[b]


def kernel(
    density_hbm,
    pattern_hbm,
    out_ref,
    density,
    pattern,
    kept,
    left,
    packed,
    incoming,
    total_low,
    total_high,
    ship,
    landed,
    load_sems,
    credits,
    relay,
    extra,
    staged,
    partly,
    extra_sem,
    part_sems,
    around_sem,
    left_sems,
    send_sems,
    recv_sems,
    ship_sems,
):
    rows, cols = lax.axis_size("row"), lax.axis_size("col")
    a, b, z = lax.axis_index("row"), lax.axis_index("col"), lax.axis_index("depth")
    other = 1 - z
    size = density.shape[-1]

    def load(first, count, sem):
        return pltpu.make_async_copy(
            density_hbm.at[0, pl.ds(first, count), pl.ds(1 - z, 2)],
            density.at[pl.ds(first, count)],
            load_sems.at[sem],
        )

    load_pattern = pltpu.make_async_copy(pattern_hbm, pattern, load_sems.at[0])
    load_first, load_rest = load(4, 5, 1), load(0, 4, 2)
    for copy in (load_pattern, load_first, load_rest):
        copy.start()

    last, end = rows - 1, cols - 1
    last_row, first_row = a == last, a == 0
    meeting = first_row & (b == 0)
    row_of = {-1: jnp.where(last_row, 0, a + 1), 0: a, 1: jnp.where(first_row, last, a - 1)}
    col_of = {-1: jnp.where(b == end, 0, b + 1), 0: b, 1: jnp.where(b == 0, end, b - 1)}

    def device(t, layer):
        step_a, step_b = STEPS[t]
        return {"row": row_of[step_a], "col": col_of[step_b], "depth": layer}

    partners = [(t, layer) for t in AWAY for layer in range(2)] + [(CENTRE, other)]
    direct = jnp.logical_not(last_row)
    is_first = first_row & (b == 0) & (z == 0)
    row_later = {
        -1: direct & (a != last - 1 if rows > 3 else a < last) & jnp.logical_not(is_first),
        1: first_row | last_row if rows > 3 else first_row,
    }
    col_later = {-1: b != end, 0: z == 0, 1: b == 0}
    later, before, late = {}, {}, {}
    for t, layer in partners:
        step_a, step_b = STEPS[t]
        key = t, 0 if t == CENTRE else layer
        to_first = jnp.bool_(False)
        if step_a == 1 or step_a == 0:
            to_first = (row_of[step_a] == 0) & (col_of[step_b] == 0)
            to_first = to_first & (layer == 0)
        if step_a == 0:
            after = direct & ((col_later[step_b] & jnp.logical_not(is_first)) | to_first)
            ahead = direct & jnp.logical_not(after)
        else:
            after = row_later[step_a] | to_first
            ahead = jnp.logical_not(after)
        later[key], before[key], late[key] = after, ahead, to_first

    def is_later(t, layer):
        return later[t, 0 if t == CENTRE else layer]

    def is_earlier(t, layer):
        return before[t, 0 if t == CENTRE else layer]

    def credit(t, layer):
        base = {3: 1, 5: 3, 7: 6}
        if t in ROW_UP:
            return credits.at[0]
        return credits.at[5 if t == CENTRE else base[t] + layer]

    barrier = pltpu.get_barrier_semaphore()

    def greet():
        for t, layer in partners:

            @pl.when(is_later(t, layer))
            def _(t=t, layer=layer):
                pl.semaphore_signal(
                    barrier, inc=1, device_id=device(t, layer), device_id_type=MESH
                )

    def meet():
        earlier = jnp.int32(0)
        for t, layer in partners:
            earlier += is_earlier(t, layer).astype(jnp.int32)

        @pl.when(earlier > 0)
        def _():
            pl.semaphore_wait(barrier, earlier)

    @pl.when(direct)
    def _():
        greet()
        meet()
        for t, layer in partners:
            if 8 - t not in SENT:
                continue

            @pl.when(is_earlier(t, layer))
            def _(t=t, layer=layer):
                pl.semaphore_signal(
                    credit(8 - t, z),
                    inc=1,
                    device_id=device(t, layer),
                    device_id_type=MESH,
                )

    @pl.when(last_row)
    def _():
        meet()
        for t in ROW_UP:
            for layer in range(2):
                pl.semaphore_signal(
                    relay.at[0 if t == 1 else 1],
                    inc=1,
                    device_id=device(t, layer),
                    device_id_type=MESH,
                )

    def ready(t, layer):
        @pl.when(is_later(t, layer))
        def _():
            pl.semaphore_wait(credit(t, layer), 1)

    def copy_to(src, dst, send_sem, recv_sem, target):
        return pltpu.make_async_remote_copy(
            src_ref=src,
            dst_ref=dst,
            send_sem=send_sem,
            recv_sem=recv_sem,
            device_id=target,
            device_id_type=MESH,
        )

    def send(t, layer):
        first, count = tiles_of(t)
        return copy_to(
            packed.at[layer, pl.ds(first, count)],
            incoming.at[t, z, pl.ds(0, count)],
            send_sems.at[t],
            recv_sems.at[t],
            device(t, layer),
        )

    def keep(slots):
        for slot in slots:
            for layer in range(2):
                place = 3 * slot + 1 + layer - z
                block = density[slot, layer]
                kept[layer, slot] = jnp.where(
                    pattern[0, place] != 0, block, jnp.zeros_like(block)
                )

    def pack(tiles):
        for tile in tiles:
            for layer in range(2):
                packed[layer, tile] = jnp.concatenate(
                    [kept[layer, STEPS.index(step)] for step in TILES[tile]], axis=1
                )

    load_pattern.wait()
    load_first.wait()
    keep((4, 5, 7, 8))
    pack((6, 7))

    up = [(t, layer, send(t, layer)) for t in ROW_UP for layer in (1, 0)]
    around = [
        copy_to(
            packed.at[1 - layer, pl.ds(6, 2)],
            extra.at[z],
            around_sem,
            extra_sem,
            device(0, layer),
        )
        for layer in range(2)
    ]
    far = last_row & (b == end)

    def send_up(messages=up):
        for t, layer, copy in messages:
            copy.start()
            if t == 0:
                pl.when(far)(around[layer].start)

    def arrived(ref, sem):
        pltpu.make_async_copy(ref, ref, sem).wait()

    def sent(t):
        first, count = tiles_of(t)
        arrived(packed.at[:, pl.ds(first, count)], send_sems.at[t])

    def sent_up():
        for t in ROW_UP:
            sent(t)
        pl.when(far)(lambda: arrived(packed.at[:, pl.ds(6, 2)], around_sem))

    pl.when(last_row)(lambda: send_up(up[:1]))
    load_rest.wait()
    keep((3, 6))
    pack((5,))

    @pl.when(last_row)
    def _():
        pl.when(jnp.logical_not(far))(lambda: send_up(up[1:]))
        greet()

    keep(range(3))
    pack(range(5))
    for slot in range(9):
        left[z, slot] = jnp.concatenate([kept[0, slot], kept[1, slot]], axis=1)

    pl.when(far)(lambda: send_up(up[1:]))

    @pl.when(last_row)
    def _():
        sent_up()
        pl.semaphore_wait(relay.at[2], 1)

    sibling = device(CENTRE, other)
    swap = copy_to(left.at[z], left.at[z], left_sems.at[0], left_sems.at[1], sibling)
    near = [(t, layer, [send(t, layer)]) for t in COLUMN for layer in range(2)]
    centre = send(CENTRE, other)
    near.append((CENTRE, other, [swap, centre]))
    down = [(t, layer, send(t, layer)) for t in ROW_DOWN for layer in range(2)]

    def offer(messages, wanted):
        for t, layer, group in messages:

            @pl.when(wanted(t, layer))
            def _(t=t, layer=layer, group=group):
                ready(t, layer)
                for copy in group:
                    copy.start()

    def to_first(t, layer):
        return late[t, 0 if t == CENTRE else layer]

    downward = [(t, layer, [copy]) for t, layer, copy in down]
    offer(near, lambda t, layer: jnp.logical_not(to_first(t, layer)))
    offer(downward, lambda t, layer: (a > 0) & jnp.logical_not(to_first(t, layer)))

    @pl.when(direct)
    def _():
        awaited = jnp.int32(0)
        for t, layer, _ in up:
            awaited += is_later(t, layer).astype(jnp.int32)

        @pl.when(awaited > 0)
        def _():
            pl.semaphore_wait(credits.at[0], awaited)

        send_up()

    offer([m for m in near if m[0] == CENTRE or m[1] == 0], to_first)
    offer(downward[:1], lambda t, layer: (a > 0) & to_first(t, layer))

    def product(t):
        lhs = jnp.concatenate([left[0, t], left[1, t]], axis=0)
        tiles = [
            jnp.concatenate([incoming[t, 0, j], incoming[t, 1, j]], axis=0)
            for j in range(tiles_of(t)[1])
        ]
        found = jnp.dot(
            lhs, jnp.concatenate(tiles, axis=1), preferred_element_type=jnp.float32
        )
        return [
            found[:, 2 * size * j : 2 * size * (j + 1)].reshape(2, size, 2 * size)
            for j in range(len(tiles))
        ]

    def receive(t):
        arrived(incoming.at[t, :, pl.ds(0, tiles_of(t)[1])], recv_sems.at[t])

    nothing = jnp.zeros((size, size), out_ref.dtype)

    def put(goal_a, goal_b, layer, block):
        place = 3 * STEPS.index((goal_a, goal_b)) + 1 + layer - z
        out_ref[0, place] = jnp.where(pattern[0, place] != 0, block, nothing)

    receive(7)
    onward = [
        copy_to(
            incoming.at[7, :, pl.ds(first, 2)],
            incoming.at[corner, :, pl.ds(0, 2)],
            send_sems.at[corner],
            recv_sems.at[corner],
            device(column, z),
        )
        for corner, column, first in ((6, 3, 1), (8, 5, 0))
    ]
    for copy in onward:
        copy.start()

    for j in range(5):
        incoming[CENTRE, z, j] = packed[z, j]
    arrived(left.at[other], left_sems.at[1])
    arrived(incoming.at[CENTRE, other], recv_sems.at[CENTRE])
    parts = product(CENTRE)
    blank = jnp.zeros((2, size, size), jnp.float32)
    for sb in range(3):
        total_low[sb] = parts[1 + sb]
    total_high[0] = jnp.concatenate([blank, parts[0][:, :, :size]], axis=2)
    total_high[1] = jnp.concatenate([blank, parts[0][:, :, size:]], axis=2)
    total_high[2] = jnp.concatenate([blank, parts[4][:, :, size:]], axis=2)
    for t in COLUMN:
        receive(t)
        parts = product(t)
        if t == 3:
            low, pair, at = parts[:2], parts[2], 0
        else:
            low, pair, at = parts[1:], parts[0], 1
        for i in range(2):
            total_low[at + i] += low[i]
        total_high[at] += jnp.concatenate([blank, pair[:, :, :size]], axis=2)
        total_high[at + 1] += jnp.concatenate([blank, pair[:, :, size:]], axis=2)

    def row_part(t, total):
        parts = product(t)
        at = {-1: 0, 0: 0, 1: 1}[STEPS[t][1]]
        for i, part in enumerate(parts):
            total[at + i] += part

    row_part(7, total_high)
    for t in (6, 8):
        receive(t)
        row_part(t, total_high)
    for sb in range(3):
        total_low[sb] += jnp.concatenate([blank, total_high[sb][:, :, :size]], axis=2)
        ship[0, sb] = total_high[sb, other].astype(ship.dtype)

    swap_first = copy_to(
        ship.at[0], landed.at[0], ship_sems.at[0, 0], ship_sems.at[0, 1], sibling
    )
    swap_first.start()

    @pl.when(a == 0)
    def _():
        pl.semaphore_wait(relay.at[0], 2)
        for _, _, copy in down:
            copy.start()

    for target in range(9):
        out_ref[0, 3 * target + 1 + z - other] = nothing
    for sb in range(3):
        own = total_high[sb, z].astype(out_ref.dtype)
        put(1, sb - 1, z, own[:, size:])

    def take(t):
        receive(t)
        row_part(t, total_low)

    @pl.when(first_row)
    def _():
        pl.semaphore_wait(relay.at[1], 4)
        pl.semaphore_signal(
            relay.at[2], inc=1, device_id=device(7, z), device_id_type=MESH
        )

    pl.when(jnp.logical_not(meeting))(lambda: take(0))
    take(2)
    take(1)

    def tidy():
        arrived(landed.at[0], ship_sems.at[0, 1])
        for sb in range(3):
            put(1, sb - 1, other, landed[0, sb][:, size:])
        pl.when(jnp.logical_not(last_row))(sent_up)
        for t in COLUMN + ROW_DOWN:
            sent(t)
        for copy in [swap, centre, swap_first] + onward:
            copy.wait_send()

    partial = copy_to(staged, partly, part_sems.at[0], part_sems.at[1], sibling)
    swap_last = copy_to(
        ship.at[1], landed.at[1], ship_sems.at[1, 0], ship_sems.at[1, 1], sibling
    )

    @pl.when(meeting)
    def _():
        for sb in range(3):
            staged[sb] = total_low[sb, other]
        partial.start()
        tidy()
        arrived(partly, part_sems.at[1])
        arrived(extra, extra_sem)
        found = jnp.dot(
            left[z, 0],
            jnp.concatenate(
                [jnp.concatenate([extra[0, j], extra[1, j]], axis=0) for j in range(2)], axis=1
            ),
            preferred_element_type=jnp.float32,
        )
        for sb in range(3):
            whole = partly[sb]
            if sb < 2:
                whole += found[:, 2 * size * sb : 2 * size * (sb + 1)]
            landed[1, sb] = whole.astype(landed.dtype)
        take(0)

    for sb in range(3):
        ship[1, sb] = total_low[sb, other].astype(ship.dtype)


    @pl.when(jnp.logical_not(meeting))
    def _():
        swap_last.start()
        tidy()

    for sb in range(3):
        own = total_low[sb, z].astype(out_ref.dtype)
        put(-1, sb - 1, z, own[:, :size])
        put(0, sb - 1, z, own[:, size:])
    pl.when(meeting)(partial.wait_send)
    pl.when(jnp.logical_not(meeting))(lambda: arrived(landed.at[1], ship_sems.at[1, 1]))
    for sb in range(3):
        put(-1, sb - 1, other, landed[1, sb][:, :size])
        put(0, sb - 1, other, landed[1, sb][:, size:])
    pl.when(jnp.logical_not(meeting))(swap_last.wait_send)


def local(density, pattern):
    size = density.shape[-1]
    kind = density.dtype
    wide = 2 * size
    return pl.pallas_call(
        kernel,
        out_shape=jax.ShapeDtypeStruct(density.shape, kind),
        in_specs=[pl.BlockSpec(memory_space=pltpu.HBM)] * 2,
        out_specs=pl.BlockSpec(memory_space=pltpu.VMEM),
        scratch_shapes=[
            pltpu.VMEM((9, 2, size, size), kind),
            pltpu.SMEM(pattern.shape, pattern.dtype),
            pltpu.VMEM((2, 9, size, size), kind),
            pltpu.VMEM((2, 9, size, wide), kind),
            pltpu.VMEM((2, len(TILES), size, wide), kind),
            pltpu.VMEM((9, 2, 5, size, wide), kind),
            pltpu.VMEM((3, 2, size, wide), jnp.float32),
            pltpu.VMEM((3, 2, size, wide), jnp.float32),
            pltpu.VMEM((2, 3, size, wide), kind),
            pltpu.VMEM((2, 3, size, wide), kind),
            pltpu.SemaphoreType.DMA((3,)),
            pltpu.SemaphoreType.REGULAR((8,)),
            pltpu.SemaphoreType.REGULAR((3,)),
            pltpu.VMEM((2, 2, size, wide), kind),
            pltpu.VMEM((3, size, wide), jnp.float32),
            pltpu.VMEM((3, size, wide), jnp.float32),
            pltpu.SemaphoreType.DMA,
            pltpu.SemaphoreType.DMA((2,)),
            pltpu.SemaphoreType.DMA,
            pltpu.SemaphoreType.DMA((2,)),
            pltpu.SemaphoreType.DMA((9,)),
            pltpu.SemaphoreType.DMA((9,)),
            pltpu.SemaphoreType.DMA((2, 2)),
        ],
        compiler_params=pltpu.CompilerParams(
            collective_id=0,
            has_side_effects=True,
            vmem_limit_bytes=32 * 1024 * 1024,
        ),
    )(
        pltpu.with_memory_space_constraint(
            density.reshape(1, 9, 3, size, size), pltpu.HBM
        ),
        pltpu.with_memory_space_constraint(pattern, pltpu.HBM),
    )


def solution(mesh):
    placed = (P(("row", "col", "depth"), None, None, None), P(("row", "col", "depth"), None))
    return jax.shard_map(
        local,
        mesh=mesh,
        in_specs=placed,
        out_specs=P(("row", "col", "depth"), None, None, None),
        check_vma=False,
    )
```

```python
import jax
import jax.numpy as jnp
from jax import lax
from jax.experimental import pallas as pl
from jax.experimental.pallas import tpu as pltpu
from jax.sharding import PartitionSpec as P

MESH = pl.DeviceIdType.MESH
STEPS = [(a, b) for a in (-1, 0, 1) for b in (-1, 0, 1)]
CENTRE = 4
ROW_UP = [0, 2, 1]
COLUMN = [3, 5]
ROW_DOWN = [7]
SENT = ROW_UP + COLUMN + ROW_DOWN + [CENTRE]
AWAY = [0, 1, 2, 3, 5, 6, 7, 8]

TILES = [
    ((1, -1), (1, 0)),
    ((-1, -1), (0, -1)),
    ((-1, 0), (0, 0)),
    ((-1, 1), (0, 1)),
    ((1, 0), (1, 1)),
    ((0, -1), (1, -1)),
    ((0, 0), (1, 0)),
    ((0, 1), (1, 1)),
]


def tiles_of(t):
    a, b = STEPS[t]
    if a == 0:
        return {-1: (2, 3), 0: (0, 5), 1: (0, 3)}[b]
    first = 5 if a == -1 else 1
    return {-1: (first + 1, 2), 0: (first, 3), 1: (first, 2)}[b]


def kernel(
    density_hbm,
    pattern_hbm,
    out_ref,
    density,
    pattern,
    kept,
    left,
    packed,
    incoming,
    total_low,
    total_high,
    ship,
    landed,
    load_sems,
    credits,
    relay,
    extra,
    staged,
    partly,
    extra_sem,
    part_sems,
    around_sem,
    left_sems,
    send_sems,
    recv_sems,
    ship_sems,
):
    rows, cols = lax.axis_size("row"), lax.axis_size("col")
    a, b, z = lax.axis_index("row"), lax.axis_index("col"), lax.axis_index("depth")
    other = 1 - z
    size = density.shape[-1]

    def load(first, count, sem):
        return pltpu.make_async_copy(
            density_hbm.at[0, pl.ds(first, count), pl.ds(1 - z, 2)],
            density.at[pl.ds(first, count)],
            load_sems.at[sem],
        )

    load_pattern = pltpu.make_async_copy(pattern_hbm, pattern, load_sems.at[0])
    load_first, load_rest = load(4, 5, 1), load(0, 4, 2)
    for copy in (load_pattern, load_first, load_rest):
        copy.start()

    last, end = rows - 1, cols - 1
    last_row, first_row = a == last, a == 0
    meeting = first_row & (b == 0)
    row_of = {-1: jnp.where(last_row, 0, a + 1), 0: a, 1: jnp.where(first_row, last, a - 1)}
    col_of = {-1: jnp.where(b == end, 0, b + 1), 0: b, 1: jnp.where(b == 0, end, b - 1)}

    def device(t, layer):
        step_a, step_b = STEPS[t]
        return {"row": row_of[step_a], "col": col_of[step_b], "depth": layer}

    partners = [(t, layer) for t in AWAY for layer in range(2)] + [(CENTRE, other)]
    direct = jnp.logical_not(last_row)
    is_first = first_row & (b == 0) & (z == 0)
    row_later = {
        -1: direct & (a != last - 1 if rows > 3 else a < last) & jnp.logical_not(is_first),
        1: first_row | last_row if rows > 3 else first_row,
    }
    col_later = {-1: b != end, 0: z == 0, 1: b == 0}
    later, before, late = {}, {}, {}
    for t, layer in partners:
        step_a, step_b = STEPS[t]
        key = t, 0 if t == CENTRE else layer
        to_first = jnp.bool_(False)
        if step_a == 1 or step_a == 0:
            to_first = (row_of[step_a] == 0) & (col_of[step_b] == 0)
            to_first = to_first & (layer == 0)
        if step_a == 0:
            after = direct & ((col_later[step_b] & jnp.logical_not(is_first)) | to_first)
            ahead = direct & jnp.logical_not(after)
        else:
            after = row_later[step_a] | to_first
            ahead = jnp.logical_not(after)
        later[key], before[key], late[key] = after, ahead, to_first

    def is_later(t, layer):
        return later[t, 0 if t == CENTRE else layer]

    def is_earlier(t, layer):
        return before[t, 0 if t == CENTRE else layer]

    def credit(t, layer):
        base = {3: 1, 5: 3, 7: 6}
        if t in ROW_UP:
            return credits.at[0]
        return credits.at[5 if t == CENTRE else base[t] + layer]

    barrier = pltpu.get_barrier_semaphore()

    def greet():
        for t, layer in partners:

            @pl.when(is_later(t, layer))
            def _(t=t, layer=layer):
                pl.semaphore_signal(
                    barrier, inc=1, device_id=device(t, layer), device_id_type=MESH
                )

    def meet():
        earlier = jnp.int32(0)
        for t, layer in partners:
            earlier += is_earlier(t, layer).astype(jnp.int32)

        @pl.when(earlier > 0)
        def _():
            pl.semaphore_wait(barrier, earlier)

    @pl.when(direct)
    def _():
        greet()
        meet()
        for t, layer in partners:
            if 8 - t not in SENT:
                continue

            @pl.when(is_earlier(t, layer))
            def _(t=t, layer=layer):
                pl.semaphore_signal(
                    credit(8 - t, z),
                    inc=1,
                    device_id=device(t, layer),
                    device_id_type=MESH,
                )

    @pl.when(last_row)
    def _():
        meet()
        for t in ROW_UP:
            for layer in range(2):
                pl.semaphore_signal(
                    relay.at[0 if t == 1 else 1],
                    inc=1,
                    device_id=device(t, layer),
                    device_id_type=MESH,
                )

    def ready(t, layer):
        @pl.when(is_later(t, layer))
        def _():
            pl.semaphore_wait(credit(t, layer), 1)

    def copy_to(src, dst, send_sem, recv_sem, target):
        return pltpu.make_async_remote_copy(
            src_ref=src,
            dst_ref=dst,
            send_sem=send_sem,
            recv_sem=recv_sem,
            device_id=target,
            device_id_type=MESH,
        )

    def send(t, layer):
        first, count = tiles_of(t)
        return copy_to(
            packed.at[layer, pl.ds(first, count)],
            incoming.at[t, z, pl.ds(0, count)],
            send_sems.at[t],
            recv_sems.at[t],
            device(t, layer),
        )

    def keep(slots):
        for slot in slots:
            for layer in range(2):
                place = 3 * slot + 1 + layer - z
                block = density[slot, layer]
                kept[layer, slot] = jnp.where(
                    pattern[0, place] != 0, block, jnp.zeros_like(block)
                )

    def pack(tiles):
        for tile in tiles:
            for layer in range(2):
                packed[layer, tile] = jnp.concatenate(
                    [kept[layer, STEPS.index(step)] for step in TILES[tile]], axis=1
                )

    load_pattern.wait()
    load_first.wait()
    keep((4, 5, 7, 8))
    pack((6, 7))

    up = [(t, layer, send(t, layer)) for t in ROW_UP for layer in (1, 0)]
    around = [
        copy_to(
            packed.at[1 - layer, pl.ds(6, 2)],
            extra.at[z],
            around_sem,
            extra_sem,
            device(0, layer),
        )
        for layer in range(2)
    ]
    far = last_row & (b == end)

    def send_up(messages=up):
        for t, layer, copy in messages:
            copy.start()
            if t == 0:
                pl.when(far)(around[layer].start)

    def arrived(ref, sem):
        pltpu.make_async_copy(ref, ref, sem).wait()

    def sent(t):
        first, count = tiles_of(t)
        arrived(packed.at[:, pl.ds(first, count)], send_sems.at[t])

    def sent_up():
        for t in ROW_UP:
            sent(t)
        pl.when(far)(lambda: arrived(packed.at[:, pl.ds(6, 2)], around_sem))

    pl.when(last_row)(lambda: send_up(up[:1]))
    load_rest.wait()
    keep((3, 6))
    pack((5,))

    @pl.when(last_row)
    def _():
        pl.when(jnp.logical_not(far))(lambda: send_up(up[1:]))
        greet()

    keep(range(3))
    pack(range(5))
    for slot in range(9):
        left[z, slot] = jnp.concatenate([kept[0, slot], kept[1, slot]], axis=1)

    pl.when(far)(lambda: send_up(up[2:] + up[1:2]))

    @pl.when(last_row)
    def _():
        sent_up()
        pl.semaphore_wait(relay.at[2], 1)

    sibling = device(CENTRE, other)
    swap = copy_to(left.at[z], left.at[z], left_sems.at[0], left_sems.at[1], sibling)
    near = [(t, layer, [send(t, layer)]) for t in COLUMN for layer in range(2)]
    centre = send(CENTRE, other)
    near.append((CENTRE, other, [swap, centre]))
    down = [(t, layer, send(t, layer)) for t in ROW_DOWN for layer in range(2)]

    def offer(messages, wanted):
        for t, layer, group in messages:

            @pl.when(wanted(t, layer))
            def _(t=t, layer=layer, group=group):
                ready(t, layer)
                for copy in group:
                    copy.start()

    def to_first(t, layer):
        return late[t, 0 if t == CENTRE else layer]

    downward = [(t, layer, [copy]) for t, layer, copy in down]
    offer(near, lambda t, layer: jnp.logical_not(to_first(t, layer)))
    offer(downward, lambda t, layer: (a > 0) & jnp.logical_not(to_first(t, layer)))

    @pl.when(direct)
    def _():
        awaited = jnp.int32(0)
        for t, layer, _ in up:
            awaited += is_later(t, layer).astype(jnp.int32)

        @pl.when(awaited > 0)
        def _():
            pl.semaphore_wait(credits.at[0], awaited)

        send_up()

    offer([m for m in near if m[0] == CENTRE or m[1] == 0], to_first)
    offer(downward[:1], lambda t, layer: (a > 0) & to_first(t, layer))

    def product(t):
        lhs = jnp.concatenate([left[0, t], left[1, t]], axis=0)
        tiles = [
            jnp.concatenate([incoming[t, 0, j], incoming[t, 1, j]], axis=0)
            for j in range(tiles_of(t)[1])
        ]
        found = jnp.dot(
            lhs, jnp.concatenate(tiles, axis=1), preferred_element_type=jnp.float32
        )
        return [
            found[:, 2 * size * j : 2 * size * (j + 1)].reshape(2, size, 2 * size)
            for j in range(len(tiles))
        ]

    def receive(t):
        arrived(incoming.at[t, :, pl.ds(0, tiles_of(t)[1])], recv_sems.at[t])

    nothing = jnp.zeros((size, size), out_ref.dtype)

    def put(goal_a, goal_b, layer, block):
        place = 3 * STEPS.index((goal_a, goal_b)) + 1 + layer - z
        out_ref[0, place] = jnp.where(pattern[0, place] != 0, block, nothing)

    receive(7)
    onward = [
        copy_to(
            incoming.at[7, :, pl.ds(first, 2)],
            incoming.at[corner, :, pl.ds(0, 2)],
            send_sems.at[corner],
            recv_sems.at[corner],
            device(column, z),
        )
        for corner, column, first in ((6, 3, 1), (8, 5, 0))
    ]
    for copy in onward:
        copy.start()

    for j in range(5):
        incoming[CENTRE, z, j] = packed[z, j]
    arrived(left.at[other], left_sems.at[1])
    arrived(incoming.at[CENTRE, other], recv_sems.at[CENTRE])
    parts = product(CENTRE)
    blank = jnp.zeros((2, size, size), jnp.float32)
    for sb in range(3):
        total_low[sb] = parts[1 + sb]
    total_high[0] = jnp.concatenate([blank, parts[0][:, :, :size]], axis=2)
    total_high[1] = jnp.concatenate([blank, parts[0][:, :, size:]], axis=2)
    total_high[2] = jnp.concatenate([blank, parts[4][:, :, size:]], axis=2)
    for t in COLUMN:
        receive(t)
        parts = product(t)
        if t == 3:
            low, pair, at = parts[:2], parts[2], 0
        else:
            low, pair, at = parts[1:], parts[0], 1
        for i in range(2):
            total_low[at + i] += low[i]
        total_high[at] += jnp.concatenate([blank, pair[:, :, :size]], axis=2)
        total_high[at + 1] += jnp.concatenate([blank, pair[:, :, size:]], axis=2)

    def row_part(t, total):
        parts = product(t)
        at = {-1: 0, 0: 0, 1: 1}[STEPS[t][1]]
        for i, part in enumerate(parts):
            total[at + i] += part

    row_part(7, total_high)
    for t in (6, 8):
        receive(t)
        row_part(t, total_high)
    for sb in range(3):
        total_low[sb] += jnp.concatenate([blank, total_high[sb][:, :, :size]], axis=2)
        ship[0, sb] = total_high[sb, other].astype(ship.dtype)

    swap_first = copy_to(
        ship.at[0], landed.at[0], ship_sems.at[0, 0], ship_sems.at[0, 1], sibling
    )
    swap_first.start()

    @pl.when(a == 0)
    def _():
        pl.semaphore_wait(relay.at[0], 2)
        for _, _, copy in down:
            copy.start()

    for target in range(9):
        out_ref[0, 3 * target + 1 + z - other] = nothing
    for sb in range(3):
        own = total_high[sb, z].astype(out_ref.dtype)
        put(1, sb - 1, z, own[:, size:])

    def take(t):
        receive(t)
        row_part(t, total_low)

    @pl.when(first_row)
    def _():
        pl.semaphore_wait(relay.at[1], 4)
        pl.semaphore_signal(
            relay.at[2], inc=1, device_id=device(7, z), device_id_type=MESH
        )

    pl.when(jnp.logical_not(meeting))(lambda: take(0))
    take(2)
    take(1)

    def tidy():
        arrived(landed.at[0], ship_sems.at[0, 1])
        for sb in range(3):
            put(1, sb - 1, other, landed[0, sb][:, size:])
        pl.when(jnp.logical_not(last_row))(sent_up)
        for t in COLUMN + ROW_DOWN:
            sent(t)
        for copy in [swap, centre, swap_first] + onward:
            copy.wait_send()

    partial = copy_to(staged, partly, part_sems.at[0], part_sems.at[1], sibling)
    swap_last = copy_to(
        ship.at[1], landed.at[1], ship_sems.at[1, 0], ship_sems.at[1, 1], sibling
    )

    @pl.when(meeting)
    def _():
        for sb in range(3):
            staged[sb] = total_low[sb, other]
        partial.start()
        tidy()
        arrived(partly, part_sems.at[1])
        arrived(extra, extra_sem)
        receive(0)
        found = jnp.dot(
            left[z, 0],
            jnp.concatenate(
                [jnp.concatenate([extra[0, j], extra[1, j]], axis=0) for j in range(2)], axis=1
            ),
            preferred_element_type=jnp.float32,
        )
        for sb in range(3):
            whole = partly[sb]
            if sb < 2:
                whole += found[:, 2 * size * sb : 2 * size * (sb + 1)]
            landed[1, sb] = whole.astype(landed.dtype)
        row_part(0, total_low)

    for sb in range(3):
        ship[1, sb] = total_low[sb, other].astype(ship.dtype)


    @pl.when(jnp.logical_not(meeting))
    def _():
        swap_last.start()
        tidy()

    for sb in range(3):
        own = total_low[sb, z].astype(out_ref.dtype)
        put(-1, sb - 1, z, own[:, :size])
        put(0, sb - 1, z, own[:, size:])
    pl.when(meeting)(partial.wait_send)
    pl.when(jnp.logical_not(meeting))(lambda: arrived(landed.at[1], ship_sems.at[1, 1]))
    for sb in range(3):
        put(-1, sb - 1, other, landed[1, sb][:, :size])
        put(0, sb - 1, other, landed[1, sb][:, size:])
    pl.when(jnp.logical_not(meeting))(swap_last.wait_send)


def local(density, pattern):
    size = density.shape[-1]
    kind = density.dtype
    wide = 2 * size
    return pl.pallas_call(
        kernel,
        out_shape=jax.ShapeDtypeStruct(density.shape, kind),
        in_specs=[pl.BlockSpec(memory_space=pltpu.HBM)] * 2,
        out_specs=pl.BlockSpec(memory_space=pltpu.VMEM),
        scratch_shapes=[
            pltpu.VMEM((9, 2, size, size), kind),
            pltpu.SMEM(pattern.shape, pattern.dtype),
            pltpu.VMEM((2, 9, size, size), kind),
            pltpu.VMEM((2, 9, size, wide), kind),
            pltpu.VMEM((2, len(TILES), size, wide), kind),
            pltpu.VMEM((9, 2, 5, size, wide), kind),
            pltpu.VMEM((3, 2, size, wide), jnp.float32),
            pltpu.VMEM((3, 2, size, wide), jnp.float32),
            pltpu.VMEM((2, 3, size, wide), kind),
            pltpu.VMEM((2, 3, size, wide), kind),
            pltpu.SemaphoreType.DMA((3,)),
            pltpu.SemaphoreType.REGULAR((8,)),
            pltpu.SemaphoreType.REGULAR((3,)),
            pltpu.VMEM((2, 2, size, wide), kind),
            pltpu.VMEM((3, size, wide), jnp.float32),
            pltpu.VMEM((3, size, wide), jnp.float32),
            pltpu.SemaphoreType.DMA,
            pltpu.SemaphoreType.DMA((2,)),
            pltpu.SemaphoreType.DMA,
            pltpu.SemaphoreType.DMA((2,)),
            pltpu.SemaphoreType.DMA((9,)),
            pltpu.SemaphoreType.DMA((9,)),
            pltpu.SemaphoreType.DMA((2, 2)),
        ],
        compiler_params=pltpu.CompilerParams(
            collective_id=0,
            has_side_effects=True,
            vmem_limit_bytes=32 * 1024 * 1024,
        ),
    )(
        pltpu.with_memory_space_constraint(
            density.reshape(1, 9, 3, size, size), pltpu.HBM
        ),
        pltpu.with_memory_space_constraint(pattern, pltpu.HBM),
    )


def solution(mesh):
    placed = (P(("row", "col", "depth"), None, None, None), P(("row", "col", "depth"), None))
    return jax.shard_map(
        local,
        mesh=mesh,
        in_specs=placed,
        out_specs=P(("row", "col", "depth"), None, None, None),
        check_vma=False,
    )
```

```python
import jax
import jax.numpy as jnp
from jax import lax
from jax.experimental import pallas as pl
from jax.experimental.pallas import tpu as pltpu
from jax.sharding import PartitionSpec as P

MESH = pl.DeviceIdType.MESH
STEPS = [(a, b) for a in (-1, 0, 1) for b in (-1, 0, 1)]
CENTRE = 4
ROW_UP = [0, 2, 1]
COLUMN = [3, 5]
ROW_DOWN = [7]
SENT = ROW_UP + COLUMN + ROW_DOWN + [CENTRE]
AWAY = [0, 1, 2, 3, 5, 6, 7, 8]

TILES = [
    ((1, -1), (1, 0)),
    ((-1, -1), (0, -1)),
    ((-1, 0), (0, 0)),
    ((-1, 1), (0, 1)),
    ((1, 0), (1, 1)),
    ((0, -1), (1, -1)),
    ((0, 0), (1, 0)),
    ((0, 1), (1, 1)),
]


def tiles_of(t):
    a, b = STEPS[t]
    if a == 0:
        return {-1: (2, 3), 0: (0, 5), 1: (0, 3)}[b]
    first = 5 if a == -1 else 1
    return {-1: (first + 1, 2), 0: (first, 3), 1: (first, 2)}[b]


def kernel(
    density_hbm,
    pattern_hbm,
    out_ref,
    density,
    pattern,
    kept,
    left,
    packed,
    incoming,
    total_low,
    total_high,
    ship,
    landed,
    load_sems,
    credits,
    relay,
    extra,
    staged,
    partly,
    extra_sem,
    part_sems,
    around_sem,
    left_sems,
    send_sems,
    recv_sems,
    ship_sems,
):
    rows, cols = lax.axis_size("row"), lax.axis_size("col")
    a, b, z = lax.axis_index("row"), lax.axis_index("col"), lax.axis_index("depth")
    other = 1 - z
    size = density.shape[-1]

    def load(first, count, sem):
        return pltpu.make_async_copy(
            density_hbm.at[0, pl.ds(first, count), pl.ds(1 - z, 2)],
            density.at[pl.ds(first, count)],
            load_sems.at[sem],
        )

    load_pattern = pltpu.make_async_copy(pattern_hbm, pattern, load_sems.at[0])
    load_first = [load(4, 2, 1), load(7, 2, 1)]
    for copy in [load_pattern] + load_first:
        copy.start()

    last, end = rows - 1, cols - 1
    last_row, first_row = a == last, a == 0
    meeting = first_row & (b == 0)
    row_of = {-1: jnp.where(last_row, 0, a + 1), 0: a, 1: jnp.where(first_row, last, a - 1)}
    col_of = {-1: jnp.where(b == end, 0, b + 1), 0: b, 1: jnp.where(b == 0, end, b - 1)}

    def device(t, layer):
        step_a, step_b = STEPS[t]
        return {"row": row_of[step_a], "col": col_of[step_b], "depth": layer}

    partners = [(t, layer) for t in AWAY for layer in range(2)] + [(CENTRE, other)]
    direct = jnp.logical_not(last_row)
    is_first = first_row & (b == 0) & (z == 0)
    row_later = {
        -1: direct & (a != last - 1 if rows > 3 else a < last) & jnp.logical_not(is_first),
        1: first_row | last_row if rows > 3 else first_row,
    }
    col_later = {-1: b != end, 0: z == 0, 1: b == 0}
    later, before, late = {}, {}, {}
    for t, layer in partners:
        step_a, step_b = STEPS[t]
        key = t, 0 if t == CENTRE else layer
        to_first = jnp.bool_(False)
        if step_a == 1 or step_a == 0:
            to_first = (row_of[step_a] == 0) & (col_of[step_b] == 0)
            to_first = to_first & (layer == 0)
        if step_a == 0:
            after = direct & ((col_later[step_b] & jnp.logical_not(is_first)) | to_first)
            ahead = direct & jnp.logical_not(after)
        else:
            after = row_later[step_a] | to_first
            ahead = jnp.logical_not(after)
        later[key], before[key], late[key] = after, ahead, to_first

    def is_later(t, layer):
        return later[t, 0 if t == CENTRE else layer]

    def is_earlier(t, layer):
        return before[t, 0 if t == CENTRE else layer]

    def credit(t, layer):
        base = {3: 1, 5: 3, 7: 6}
        if t in ROW_UP:
            return credits.at[0]
        return credits.at[5 if t == CENTRE else base[t] + layer]

    barrier = pltpu.get_barrier_semaphore()

    def greet():
        for t, layer in partners:

            @pl.when(is_later(t, layer))
            def _(t=t, layer=layer):
                pl.semaphore_signal(
                    barrier, inc=1, device_id=device(t, layer), device_id_type=MESH
                )

    def meet():
        earlier = jnp.int32(0)
        for t, layer in partners:
            earlier += is_earlier(t, layer).astype(jnp.int32)

        @pl.when(earlier > 0)
        def _():
            pl.semaphore_wait(barrier, earlier)

    @pl.when(direct)
    def _():
        greet()
        meet()
        for t, layer in partners:
            if 8 - t not in SENT:
                continue

            @pl.when(is_earlier(t, layer))
            def _(t=t, layer=layer):
                pl.semaphore_signal(
                    credit(8 - t, z),
                    inc=1,
                    device_id=device(t, layer),
                    device_id_type=MESH,
                )

    @pl.when(last_row)
    def _():
        meet()
        for t in ROW_UP:
            for layer in range(2):
                pl.semaphore_signal(
                    relay.at[0 if t == 1 else 1],
                    inc=1,
                    device_id=device(t, layer),
                    device_id_type=MESH,
                )

    def ready(t, layer):
        @pl.when(is_later(t, layer))
        def _():
            pl.semaphore_wait(credit(t, layer), 1)

    def copy_to(src, dst, send_sem, recv_sem, target):
        return pltpu.make_async_remote_copy(
            src_ref=src,
            dst_ref=dst,
            send_sem=send_sem,
            recv_sem=recv_sem,
            device_id=target,
            device_id_type=MESH,
        )

    def send(t, layer):
        first, count = tiles_of(t)
        return copy_to(
            packed.at[layer, pl.ds(first, count)],
            incoming.at[t, z, pl.ds(0, count)],
            send_sems.at[t],
            recv_sems.at[t],
            device(t, layer),
        )

    def keep(slots):
        for slot in slots:
            for layer in range(2):
                place = 3 * slot + 1 + layer - z
                block = density[slot, layer]
                kept[layer, slot] = jnp.where(
                    pattern[0, place] != 0, block, jnp.zeros_like(block)
                )

    def pack(tiles):
        for tile in tiles:
            for layer in range(2):
                packed[layer, tile] = jnp.concatenate(
                    [kept[layer, STEPS.index(step)] for step in TILES[tile]], axis=1
                )

    load_pattern.wait()
    whole = density.at[pl.ds(0, 4)]
    pltpu.make_async_copy(whole, whole, load_sems.at[1]).wait()
    load_rest = [load(3, 1, 2), load(6, 1, 2), load(0, 3, 2)]
    for copy in load_rest:
        copy.start()
    keep((4, 5, 7, 8))
    pack((6, 7))

    up = [(t, layer, send(t, layer)) for t in ROW_UP for layer in (1, 0)]
    around = [
        copy_to(
            packed.at[1 - layer, pl.ds(6, 2)],
            extra.at[z],
            around_sem,
            extra_sem,
            device(0, layer),
        )
        for layer in range(2)
    ]
    far = last_row & (b == end)

    def send_up(messages=up):
        for t, layer, copy in messages:
            copy.start()
            if t == 0:
                pl.when(far)(around[layer].start)

    def arrived(ref, sem):
        pltpu.make_async_copy(ref, ref, sem).wait()

    def sent(t):
        first, count = tiles_of(t)
        arrived(packed.at[:, pl.ds(first, count)], send_sems.at[t])

    def sent_up():
        for t in ROW_UP:
            sent(t)
        pl.when(far)(lambda: arrived(packed.at[:, pl.ds(6, 2)], around_sem))

    pl.when(last_row)(lambda: send_up(up[:1]))
    whole = density.at[pl.ds(0, 5)]
    pltpu.make_async_copy(whole, whole, load_sems.at[2]).wait()
    keep((3, 6))
    pack((5,))

    @pl.when(last_row)
    def _():
        pl.when(jnp.logical_not(far))(lambda: send_up(up[1:]))
        greet()

    keep(range(3))
    pack(range(5))
    for slot in range(9):
        left[z, slot] = jnp.concatenate([kept[0, slot], kept[1, slot]], axis=1)

    pl.when(far)(lambda: send_up(up[2:] + up[1:2]))

    @pl.when(last_row)
    def _():
        sent_up()
        pl.semaphore_wait(relay.at[2], 1)

    sibling = device(CENTRE, other)
    swap = copy_to(left.at[z], left.at[z], left_sems.at[0], left_sems.at[1], sibling)
    near = [(t, layer, [send(t, layer)]) for t in COLUMN for layer in range(2)]
    centre = send(CENTRE, other)
    near.append((CENTRE, other, [swap, centre]))
    down = [(t, layer, send(t, layer)) for t in ROW_DOWN for layer in range(2)]

    def offer(messages, wanted):
        for t, layer, group in messages:

            @pl.when(wanted(t, layer))
            def _(t=t, layer=layer, group=group):
                ready(t, layer)
                for copy in group:
                    copy.start()

    def to_first(t, layer):
        return late[t, 0 if t == CENTRE else layer]

    downward = [(t, layer, [copy]) for t, layer, copy in down]
    offer(near, lambda t, layer: jnp.logical_not(to_first(t, layer)))
    offer(downward, lambda t, layer: (a > 0) & jnp.logical_not(to_first(t, layer)))

    @pl.when(direct)
    def _():
        awaited = jnp.int32(0)
        for t, layer, _ in up:
            awaited += is_later(t, layer).astype(jnp.int32)

        @pl.when(awaited > 0)
        def _():
            pl.semaphore_wait(credits.at[0], awaited)

        send_up()

    offer([m for m in near if m[0] == CENTRE or m[1] == 0], to_first)
    offer(downward[:1], lambda t, layer: (a > 0) & to_first(t, layer))

    def product(t):
        lhs = jnp.concatenate([left[0, t], left[1, t]], axis=0)
        tiles = [
            jnp.concatenate([incoming[t, 0, j], incoming[t, 1, j]], axis=0)
            for j in range(tiles_of(t)[1])
        ]
        found = jnp.dot(
            lhs, jnp.concatenate(tiles, axis=1), preferred_element_type=jnp.float32
        )
        return [
            found[:, 2 * size * j : 2 * size * (j + 1)].reshape(2, size, 2 * size)
            for j in range(len(tiles))
        ]

    def receive(t):
        arrived(incoming.at[t, :, pl.ds(0, tiles_of(t)[1])], recv_sems.at[t])

    nothing = jnp.zeros((size, size), out_ref.dtype)

    def put(goal_a, goal_b, layer, block):
        place = 3 * STEPS.index((goal_a, goal_b)) + 1 + layer - z
        out_ref[0, place] = jnp.where(pattern[0, place] != 0, block, nothing)

    receive(7)
    onward = [
        copy_to(
            incoming.at[7, :, pl.ds(first, 2)],
            incoming.at[corner, :, pl.ds(0, 2)],
            send_sems.at[corner],
            recv_sems.at[corner],
            device(column, z),
        )
        for corner, column, first in ((6, 3, 1), (8, 5, 0))
    ]
    for copy in onward:
        copy.start()

    for j in range(5):
        incoming[CENTRE, z, j] = packed[z, j]
    arrived(left.at[other], left_sems.at[1])
    arrived(incoming.at[CENTRE, other], recv_sems.at[CENTRE])
    parts = product(CENTRE)
    blank = jnp.zeros((2, size, size), jnp.float32)
    for sb in range(3):
        total_low[sb] = parts[1 + sb]
    total_high[0] = jnp.concatenate([blank, parts[0][:, :, :size]], axis=2)
    total_high[1] = jnp.concatenate([blank, parts[0][:, :, size:]], axis=2)
    total_high[2] = jnp.concatenate([blank, parts[4][:, :, size:]], axis=2)
    for t in COLUMN:
        receive(t)
        parts = product(t)
        if t == 3:
            low, pair, at = parts[:2], parts[2], 0
        else:
            low, pair, at = parts[1:], parts[0], 1
        for i in range(2):
            total_low[at + i] += low[i]
        total_high[at] += jnp.concatenate([blank, pair[:, :, :size]], axis=2)
        total_high[at + 1] += jnp.concatenate([blank, pair[:, :, size:]], axis=2)

    def row_part(t, total):
        parts = product(t)
        at = {-1: 0, 0: 0, 1: 1}[STEPS[t][1]]
        for i, part in enumerate(parts):
            total[at + i] += part

    row_part(7, total_high)
    for t in (6, 8):
        receive(t)
        row_part(t, total_high)
    for sb in range(3):
        total_low[sb] += jnp.concatenate([blank, total_high[sb][:, :, :size]], axis=2)
        ship[0, sb] = total_high[sb, other].astype(ship.dtype)

    swap_first = copy_to(
        ship.at[0], landed.at[0], ship_sems.at[0, 0], ship_sems.at[0, 1], sibling
    )
    swap_first.start()

    @pl.when(a == 0)
    def _():
        pl.semaphore_wait(relay.at[0], 2)
        for _, _, copy in down:
            copy.start()

    for target in range(9):
        out_ref[0, 3 * target + 1 + z - other] = nothing
    for sb in range(3):
        own = total_high[sb, z].astype(out_ref.dtype)
        put(1, sb - 1, z, own[:, size:])

    def take(t):
        receive(t)
        row_part(t, total_low)

    @pl.when(first_row)
    def _():
        pl.semaphore_wait(relay.at[1], 4)
        pl.semaphore_signal(
            relay.at[2], inc=1, device_id=device(7, z), device_id_type=MESH
        )

    pl.when(jnp.logical_not(meeting))(lambda: take(0))
    take(2)
    take(1)

    def tidy():
        arrived(landed.at[0], ship_sems.at[0, 1])
        for sb in range(3):
            put(1, sb - 1, other, landed[0, sb][:, size:])
        pl.when(jnp.logical_not(last_row))(sent_up)
        for t in COLUMN + ROW_DOWN:
            sent(t)
        for copy in [swap, centre, swap_first] + onward:
            copy.wait_send()

    partial = copy_to(staged, partly, part_sems.at[0], part_sems.at[1], sibling)
    swap_last = copy_to(
        ship.at[1], landed.at[1], ship_sems.at[1, 0], ship_sems.at[1, 1], sibling
    )

    @pl.when(meeting)
    def _():
        for sb in range(3):
            staged[sb] = total_low[sb, other]
        partial.start()
        tidy()
        arrived(partly, part_sems.at[1])
        arrived(extra, extra_sem)
        receive(0)
        found = jnp.dot(
            left[z, 0],
            jnp.concatenate(
                [jnp.concatenate([extra[0, j], extra[1, j]], axis=0) for j in range(2)], axis=1
            ),
            preferred_element_type=jnp.float32,
        )
        for sb in range(3):
            whole = partly[sb]
            if sb < 2:
                whole += found[:, 2 * size * sb : 2 * size * (sb + 1)]
            landed[1, sb] = whole.astype(landed.dtype)
        row_part(0, total_low)

    for sb in range(3):
        ship[1, sb] = total_low[sb, other].astype(ship.dtype)


    @pl.when(jnp.logical_not(meeting))
    def _():
        swap_last.start()
        tidy()

    for sb in range(3):
        own = total_low[sb, z].astype(out_ref.dtype)
        put(-1, sb - 1, z, own[:, :size])
        put(0, sb - 1, z, own[:, size:])
    pl.when(meeting)(partial.wait_send)
    pl.when(jnp.logical_not(meeting))(lambda: arrived(landed.at[1], ship_sems.at[1, 1]))
    for sb in range(3):
        put(-1, sb - 1, other, landed[1, sb][:, :size])
        put(0, sb - 1, other, landed[1, sb][:, size:])
    pl.when(jnp.logical_not(meeting))(swap_last.wait_send)


def local(density, pattern):
    size = density.shape[-1]
    kind = density.dtype
    wide = 2 * size
    return pl.pallas_call(
        kernel,
        out_shape=jax.ShapeDtypeStruct(density.shape, kind),
        in_specs=[pl.BlockSpec(memory_space=pltpu.HBM)] * 2,
        out_specs=pl.BlockSpec(memory_space=pltpu.VMEM),
        scratch_shapes=[
            pltpu.VMEM((9, 2, size, size), kind),
            pltpu.SMEM(pattern.shape, pattern.dtype),
            pltpu.VMEM((2, 9, size, size), kind),
            pltpu.VMEM((2, 9, size, wide), kind),
            pltpu.VMEM((2, len(TILES), size, wide), kind),
            pltpu.VMEM((9, 2, 5, size, wide), kind),
            pltpu.VMEM((3, 2, size, wide), jnp.float32),
            pltpu.VMEM((3, 2, size, wide), jnp.float32),
            pltpu.VMEM((2, 3, size, wide), kind),
            pltpu.VMEM((2, 3, size, wide), kind),
            pltpu.SemaphoreType.DMA((3,)),
            pltpu.SemaphoreType.REGULAR((8,)),
            pltpu.SemaphoreType.REGULAR((3,)),
            pltpu.VMEM((2, 2, size, wide), kind),
            pltpu.VMEM((3, size, wide), jnp.float32),
            pltpu.VMEM((3, size, wide), jnp.float32),
            pltpu.SemaphoreType.DMA,
            pltpu.SemaphoreType.DMA((2,)),
            pltpu.SemaphoreType.DMA,
            pltpu.SemaphoreType.DMA((2,)),
            pltpu.SemaphoreType.DMA((9,)),
            pltpu.SemaphoreType.DMA((9,)),
            pltpu.SemaphoreType.DMA((2, 2)),
        ],
        compiler_params=pltpu.CompilerParams(
            collective_id=0,
            has_side_effects=True,
            vmem_limit_bytes=32 * 1024 * 1024,
        ),
    )(
        pltpu.with_memory_space_constraint(
            density.reshape(1, 9, 3, size, size), pltpu.HBM
        ),
        pltpu.with_memory_space_constraint(pattern, pltpu.HBM),
    )


def solution(mesh):
    placed = (P(("row", "col", "depth"), None, None, None), P(("row", "col", "depth"), None))
    return jax.shard_map(
        local,
        mesh=mesh,
        in_specs=placed,
        out_specs=P(("row", "col", "depth"), None, None, None),
        check_vma=False,
    )
```
